32 devices in a mesh: wide: 8 (over z, x), narrow: 4 (over y, core).
Axes of the slice: x: 2, y: 2, z: 4, core: 2. Of those that a mesh axis runs over, the one named last changes fastest.
Arguments:
- dosage: bfloat16 [32768, 4096], P(('wide', 'narrow')), may hold values from 0 to 2
- keep_rows: int32 [28672], P(('wide', 'narrow')), may hold values from 0 to 1023, as said below
- allele_counts: int32 [4096], replicated, may hold values from 19660 to 45874, as said below
- projection: bfloat16 [4096, 128], replicated, may hold values from -0.09375 to 0.09375
Outputs:
- scores: float32 [28672, 128], P(('wide', 'narrow'))
- loadings: float32 [4096, 128], P('narrow')
The draws below stay inside these ranges and needn't reach their ends.
Inputs may be any that keep to these rules, and one draw needn't show every extreme that they name: `keep_rows`: each block of 896 entries holds distinct local row numbers of one device's 1024 samples, ascending. `allele_counts`: totals over all 32768 genotyped samples, before outlier removal.
All inputs are finite; a program needn't handle non-finite values.
Results may differ from the reference program's by a relative error of at most 0.0075.
The reference program's roundings to bfloat16 on the way count: a program that leaves them out, or rounds other values in their place, can miss the bound.
Values sent between devices are 32-bit elements; how exact they have to be, the bound alone decides.
No kernel may reach another device: no remote copies, remote signals or barrier semaphores. Data moves between devices by JAX's collectives and lax.ppermute only.
A program may use at most 64 MiB of HBM per device.

```python
import math
import jax
import jax.numpy as jnp
from jax import lax

SNPS = 4096
COMPONENTS = 128
ITERS = 2
SAMP_DEV = 1024
KEEP_DEV = 896
BLOCKS = 32
NARROW_BLOCKS = 4
SAMPLES = 32768
KEPT = 28672


def allele_draw(key):
    lowest = 3 * SAMPLES // 5
    highest = 7 * SAMPLES // 5
    counts_base = jax.random.randint(jax.random.fold_in(key, 11), (SNPS,), lowest, highest)
    first_slot = jax.random.randint(jax.random.fold_in(key, 12), (), 0, SNPS)
    shift_by = jax.random.randint(jax.random.fold_in(key, 13), (), 1, SNPS)
    second_slot = (first_slot + shift_by) % SNPS
    counts_base = counts_base.at[first_slot].set(lowest)
    counts_base = counts_base.at[second_slot].set(highest - 1)
    return counts_base.astype(jnp.int32)


def draw_allele_counts(key, part):
    return allele_draw(key)


def draw_dosage(key, part):
    counts = allele_draw(key)
    frequency = counts.astype(jnp.float32) / (2.0 * SAMPLES)
    noise_field = jnp.clip(0.5 * jax.random.normal(jax.random.fold_in(key, 22), (SAMPLES, SNPS), jnp.float32), -1.0, 1.0)
    block_index = jnp.arange(SAMPLES) // SAMP_DEV
    wide_pos = (block_index // NARROW_BLOCKS).astype(jnp.float32)
    narrow_pos = (block_index % NARROW_BLOCKS).astype(jnp.float32)
    wide_count = BLOCKS // NARROW_BLOCKS
    wide_frac = wide_pos / (wide_count - 1)
    narrow_frac = narrow_pos / (NARROW_BLOCKS - 1)
    power = (1.0 + wide_frac + narrow_frac) / 3.0
    amplitude = 0.6 * jnp.sqrt(power)
    values = 2.0 * frequency[None, :] + amplitude[:, None] * noise_field
    factors = 8
    sample_factors = jnp.clip(jax.random.normal(jax.random.fold_in(key, 41), (SAMPLES, factors), jnp.float32), -3.0, 3.0)
    snp_factors = jnp.clip(jax.random.normal(jax.random.fold_in(key, 42), (factors, SNPS), jnp.float32), -3.0, 3.0)
    for factor in range(factors):
        strength = 1.2 * 0.85 ** factor / math.sqrt(SNPS)
        values = values + sample_factors[:, factor][:, None] * (strength * snp_factors[factor])[None, :]
    return jnp.clip(values, 0.0, 2.0).astype(jnp.bfloat16)


def draw_keep_rows(key, part):
    block_keys = jax.random.split(jax.random.fold_in(key, 31), BLOCKS)

    def choose_rows(one_key):
        return jnp.sort(jax.random.permutation(one_key, SAMP_DEV)[:KEEP_DEV])
    return jax.vmap(choose_rows)(block_keys).reshape(KEPT).astype(jnp.int32)


def normal_values(own_key, dims, deviation, most, kind=jnp.bfloat16):
    return jnp.clip(deviation * jax.random.normal(own_key, dims, jnp.float32), -most, most).astype(kind)


def setup_inputs(seed: int = 0) -> dict:
    splits = jax.random.split(jax.random.key(seed), 5)
    dosage = draw_dosage(jax.random.fold_in(splits[4], 71), 0)
    keep_rows = draw_keep_rows(jax.random.fold_in(splits[4], 71), 0)
    allele_counts = draw_allele_counts(jax.random.fold_in(splits[4], 71), 0)
    projection = normal_values(splits[3], (SNPS, COMPONENTS), SNPS ** -0.5, 0.09375)
    return {"dosage": dosage, "keep_rows": keep_rows, "allele_counts": allele_counts, "projection": projection}


def standardize(dosage, keep_rows, allele_counts):
    frequency = allele_counts.astype(jnp.float32) / (2.0 * SAMPLES)
    center = 2.0 * frequency
    spread = jnp.sqrt(2.0 * frequency * (1.0 - frequency))
    blocks = dosage.reshape(BLOCKS, SAMP_DEV, SNPS)
    picks = keep_rows.reshape(BLOCKS, KEEP_DEV)

    def one_block(pair):
        block_rows, pick_rows = pair
        chosen = jnp.take(block_rows, pick_rows, axis=0)
        return ((chosen.astype(jnp.float32) - center) / spread).astype(jnp.bfloat16)
    return lax.map(one_block, (blocks, picks)).reshape(KEPT, SNPS)

def invert_factor(gram_matrix):
    lower_factor = jnp.linalg.cholesky(gram_matrix)
    unit_matrix = jnp.eye(gram_matrix.shape[0], dtype=jnp.float32)
    return jax.scipy.linalg.solve_triangular(lower_factor, unit_matrix, lower=True)

def reference(dosage, keep_rows, allele_counts, projection):
    standard = standardize(dosage, keep_rows, allele_counts)
    basis_bf = projection
    projected = None
    inverse = None
    loadings = None
    for iteration in range(ITERS):
        projected = jnp.dot(standard.astype(jnp.float32), basis_bf.astype(jnp.float32), preferred_element_type=jnp.float32).astype(jnp.bfloat16)
        gram_matrix = jnp.dot(projected.T.astype(jnp.float32), projected.astype(jnp.float32), preferred_element_type=jnp.float32)
        inverse = invert_factor(gram_matrix)
        partial_value = jnp.dot(standard.T.astype(jnp.float32), projected.astype(jnp.float32), preferred_element_type=jnp.float32)
        loadings = jnp.dot(partial_value, inverse.T, precision=lax.Precision.HIGHEST)
        basis_bf = loadings.astype(jnp.bfloat16)
    scores = jnp.dot(projected.astype(jnp.float32), inverse.T, precision=lax.Precision.HIGHEST) * math.sqrt(KEPT)
    return (scores, loadings)
```

```python
import functools
import math

import jax
import jax.numpy as jnp
from jax import lax
from jax.experimental import pallas as pl
from jax.experimental.pallas import tpu as pltpu
from jax.sharding import PartitionSpec as P

AXES = ("wide", "narrow")
TILE = 128
BLOCKS = 32
ROWS = 256
VMEM = 48 * 1024 * 1024


def split(value):
    high = value.astype(jnp.bfloat16)
    low = (value - high.astype(jnp.float32)).astype(jnp.bfloat16)
    return high, low


def product(left, right_high, right_low):
    high, low = split(left)
    dims = (((1,), (1,)), ((), ()))
    dot = functools.partial(lax.dot_general, dimension_numbers=dims, preferred_element_type=jnp.float32)
    return dot(high, right_high) + (dot(high, right_low) + dot(low, right_high))


def relative(position, core):
    first = (position >> 3) & 1
    second = (position >> 2) & 1
    core_bit = (position >> 4) & 1
    target = core ^ core_bit
    bit_x = jnp.where(target == 0, first, second)
    bit_y = jnp.where(target == 0, second, first)
    return core_bit | (bit_y << 1) | (bit_x << 2) | ((position & 3) << 3)


def block_order(device):
    position = lax.iota(jnp.int32, BLOCKS)
    owner = device ^ relative(position, device & 1)
    return (owner & 3) * 8 + ((owner >> 2) & 7)


def exchange(value, mask_of):
    count = lax.axis_size(AXES)
    return lax.ppermute(value, AXES, [(d, d ^ mask_of(d)) for d in range(count)])


def core_mask(d):
    return 1


def first_mask(d):
    return 2 if d & 1 else 4


def second_mask(d):
    return 4 if d & 1 else 2


def standard_kernel(samples_total, order, dosage, keep, counts, projection, standard, projected, turned, gram, kept, table, basis):
    step = pl.program_id(0)

    @pl.when(step == 0)
    def _():
        frequency = counts[...].astype(jnp.float32) / (2.0 * samples_total)
        table[0] = 2.0 * frequency
        table[1] = 1.0 / jnp.sqrt(2.0 * frequency * (1.0 - frequency))
        for p in range(BLOCKS):
            start = pl.multiple_of(order[p] * TILE, TILE)
            basis[p * TILE : (p + 1) * TILE, :] = projection[pl.ds(start, TILE), :]
        gram[...] = jnp.zeros_like(gram)

    rows = lax.broadcasted_iota(jnp.int32, (ROWS, TILE), 0) + step * ROWS
    found = jnp.zeros((ROWS, TILE), jnp.float32)
    for j in range(keep.shape[0]):
        found = jnp.where(rows == keep[j : j + 1, :], 1.0, found)
    found = jnp.broadcast_to(jnp.max(found, axis=1, keepdims=True), (ROWS, TILE))
    kept[...] = found
    for p in range(BLOCKS):
        block = order[p]
        center = table[0, pl.ds(block, 1), :]
        scale = table[1, pl.ds(block, 1), :]
        value = dosage[:, pl.ds(pl.multiple_of(block * TILE, TILE), TILE)].astype(jnp.float32)
        standard[:, p * TILE : (p + 1) * TILE] = ((value - center) * scale).astype(jnp.bfloat16)
    value = jnp.dot(standard[...], basis[...], preferred_element_type=jnp.float32)
    value = jnp.where(found > 0.0, value, 0.0)
    low = value.astype(jnp.bfloat16)
    low_turned = value.T.astype(jnp.bfloat16)
    projected[...] = low
    turned[...] = low_turned
    gram[...] += jnp.dot(low_turned, low, preferred_element_type=jnp.float32)


def standardize(samples_total, order, dosage, keep, counts, projection):
    samples, snps = dosage.shape
    steps = samples // ROWS
    return pl.pallas_call(
        functools.partial(standard_kernel, samples_total),
        grid_spec=pltpu.PrefetchScalarGridSpec(
            num_scalar_prefetch=1,
            grid=(steps,),
            in_specs=[
                pl.BlockSpec((ROWS, snps), lambda i, order: (i, 0)),
                pl.BlockSpec(keep.shape, lambda i, order: (0, 0)),
                pl.BlockSpec(counts.shape, lambda i, order: (0, 0)),
                pl.BlockSpec(projection.shape, lambda i, order: (0, 0)),
            ],
            out_specs=[
                pl.BlockSpec((ROWS, snps), lambda i, order: (i, 0)),
                pl.BlockSpec((ROWS, TILE), lambda i, order: (i, 0)),
                pl.BlockSpec((TILE, ROWS), lambda i, order: (0, i)),
                pl.BlockSpec((TILE, TILE), lambda i, order: (0, 0)),
                pl.BlockSpec((ROWS, TILE), lambda i, order: (i, 0)),
            ],
            scratch_shapes=[
                pltpu.VMEM((2,) + counts.shape, jnp.float32),
                pltpu.VMEM(projection.shape, jnp.bfloat16),
            ],
        ),
        out_shape=[
            jax.ShapeDtypeStruct((samples, snps), jnp.bfloat16),
            jax.ShapeDtypeStruct((samples, TILE), jnp.bfloat16),
            jax.ShapeDtypeStruct((TILE, samples), jnp.bfloat16),
            jax.ShapeDtypeStruct((TILE, TILE), jnp.float32),
            jax.ShapeDtypeStruct((samples, TILE), jnp.float32),
        ],
        compiler_params=pltpu.CompilerParams(vmem_limit_bytes=VMEM),
        cost_estimate=pl.CostEstimate(flops=2 * samples * snps * TILE, bytes_accessed=4 * samples * snps, transcendentals=0),
        name="standardize",
    )(order, dosage, keep, counts, projection)


WIDTH = 512


def totals_kernel(turned, standard, out):
    out[...] = jnp.dot(turned[...], standard[...], preferred_element_type=jnp.float32).T


def totals(turned, standard, low, high):
    samples = standard.shape[0]
    base = low * TILE // WIDTH
    count = (high - low) * TILE
    return pl.pallas_call(
        totals_kernel,
        grid=(count // WIDTH,),
        in_specs=[
            pl.BlockSpec((TILE, samples), lambda i: (0, 0)),
            pl.BlockSpec((samples, WIDTH), lambda i: (0, base + i)),
        ],
        out_specs=pl.BlockSpec((WIDTH, TILE), lambda i: (i, 0)),
        out_shape=jax.ShapeDtypeStruct((count, TILE), jnp.float32),
        compiler_params=pltpu.CompilerParams(vmem_limit_bytes=VMEM),
        cost_estimate=pl.CostEstimate(flops=2 * samples * count * TILE, bytes_accessed=2 * samples * count, transcendentals=0),
        name="totals",
    )(turned, standard)


def project_kernel(pieces, *refs):
    parts = refs[:pieces]
    inverse, standard, kept, projected, turned, gram, basis = refs[pieces:]

    @pl.when(pl.program_id(0) == 0)
    def _():
        high, low = split(inverse[...])
        start = 0
        for part in parts:
            size = part.shape[0]
            basis[start : start + size, :] = product(part[...], high, low).astype(jnp.bfloat16)
            start += size
        gram[...] = jnp.zeros_like(gram)

    value = jnp.dot(standard[...], basis[...], preferred_element_type=jnp.float32)
    value = jnp.where(kept[...] > 0.0, value, 0.0)
    low = value.astype(jnp.bfloat16)
    low_turned = value.T.astype(jnp.bfloat16)
    projected[...] = low
    turned[...] = low_turned
    gram[...] += jnp.dot(low_turned, low, preferred_element_type=jnp.float32)


def project(parts, inverse, standard, kept):
    samples, snps = standard.shape
    return pl.pallas_call(
        functools.partial(project_kernel, len(parts)),
        grid=(samples // ROWS,),
        in_specs=[pl.BlockSpec(part.shape, lambda i: (0, 0)) for part in parts]
        + [
            pl.BlockSpec((TILE, TILE), lambda i: (0, 0)),
            pl.BlockSpec((ROWS, snps), lambda i: (i, 0)),
            pl.BlockSpec((ROWS, TILE), lambda i: (i, 0)),
        ],
        out_specs=[
            pl.BlockSpec((ROWS, TILE), lambda i: (i, 0)),
            pl.BlockSpec((TILE, ROWS), lambda i: (0, i)),
            pl.BlockSpec((TILE, TILE), lambda i: (0, 0)),
        ],
        out_shape=[
            jax.ShapeDtypeStruct((samples, TILE), jnp.bfloat16),
            jax.ShapeDtypeStruct((TILE, samples), jnp.bfloat16),
            jax.ShapeDtypeStruct((TILE, TILE), jnp.float32),
        ],
        scratch_shapes=[pltpu.VMEM((snps, TILE), jnp.bfloat16)],
        compiler_params=pltpu.CompilerParams(vmem_limit_bytes=VMEM),
        cost_estimate=pl.CostEstimate(flops=2 * samples * snps * TILE, bytes_accessed=2 * samples * snps, transcendentals=0),
        name="project",
    )(*parts, inverse, standard, kept)


PANEL = 16


def inverse_kernel(gram, out, left, right):
    left[...] = gram[...]
    lanes = lax.broadcasted_iota(jnp.int32, (TILE, TILE), 1)
    subs = lax.broadcasted_iota(jnp.int32, (TILE, TILE), 0)
    right[...] = jnp.where(lanes == subs, 1.0, 0.0)
    panel_rows = lax.broadcasted_iota(jnp.int32, (PANEL, TILE), 0)
    for start in range(0, TILE, PANEL):
        stop = start + PANEL
        upper = left[start:stop, :]
        done = right[start:stop, :]
        columns = [
            jnp.broadcast_to(upper[:, start + j : start + j + 1], (PANEL, TILE)) for j in range(PANEL)
        ]
        for k in range(PANEL):
            pivot = columns[k][k : k + 1, :]
            root = lax.rsqrt(pivot)
            below = jnp.where(panel_rows > k, columns[k] * (root * root), 0.0)
            for j in range(k + 1, PANEL):
                columns[j] = columns[j] - below * columns[j][k : k + 1, :]
            factor = jnp.where(panel_rows == k, root, 1.0)
            upper = upper * factor - below * upper[k : k + 1, :]
            done = done * factor - below * done[k : k + 1, :]
        out[start:stop, :] = done
        if stop < TILE:
            both = lax.dot_general(
                upper[:, stop:] if False else upper,
                jnp.concatenate([upper, done], axis=1),
                (((0,), (0,)), ((), ())),
                precision=lax.Precision.HIGHEST,
                preferred_element_type=jnp.float32,
            )
            left[stop:, :] -= both[stop:, :TILE]
            right[stop:, :] -= both[stop:, TILE:]


def invert_factor(gram):
    return pl.pallas_call(
        inverse_kernel,
        out_shape=jax.ShapeDtypeStruct((TILE, TILE), jnp.float32),
        scratch_shapes=[pltpu.VMEM((TILE, TILE), jnp.float32), pltpu.VMEM((TILE, TILE), jnp.float32)],
        compiler_params=pltpu.CompilerParams(vmem_limit_bytes=VMEM),
        cost_estimate=pl.CostEstimate(flops=20_000_000, bytes_accessed=16_000_000, transcendentals=0),
        name="invert_factor",
    )(gram)


def scores_kernel(scale, keep, projected, inverse, scores):
    high, low = split(inverse[...])
    samples = projected.shape[0]
    lanes = lax.broadcasted_iota(jnp.int32, (TILE, samples), 1).astype(jnp.float32)
    for j in range(keep.shape[0]):
        row = jnp.broadcast_to(keep[j : j + 1, :].astype(jnp.float32), (TILE, TILE)).T
        pick = jnp.where(lanes == jnp.tile(row, (1, samples // TILE)), 1.0, 0.0).astype(jnp.bfloat16)
        chosen = jnp.dot(pick, projected[...], preferred_element_type=jnp.float32).astype(jnp.bfloat16)
        dims = (((1,), (1,)), ((), ()))
        value = lax.dot_general(chosen, high, dims, preferred_element_type=jnp.float32)
        value = value + lax.dot_general(chosen, low, dims, preferred_element_type=jnp.float32)
        scores[j * TILE : (j + 1) * TILE, :] = value * scale


def score(scale, keep, projected, inverse):
    return pl.pallas_call(
        functools.partial(scores_kernel, scale),
        out_shape=jax.ShapeDtypeStruct((keep.shape[0] * TILE, TILE), jnp.float32),
        compiler_params=pltpu.CompilerParams(vmem_limit_bytes=VMEM),
        cost_estimate=pl.CostEstimate(flops=1_000_000_000, bytes_accessed=1_000_000, transcendentals=0),
        name="score",
    )(keep, projected, inverse)


def loadings_kernel(pieces, order, *refs):
    parts = refs[:pieces]
    inverse, loadings = refs[pieces:]
    high, low = split(inverse[...])
    position = 0
    for part in parts:
        for row in range(0, part.shape[0], TILE):
            start = pl.multiple_of(order[position] * TILE, TILE)
            loadings[pl.ds(start, TILE), :] = product(part[row : row + TILE, :], high, low)
            position += 1


def load(order, parts, inverse):
    count = sum(part.shape[0] for part in parts)
    return pl.pallas_call(
        functools.partial(loadings_kernel, len(parts)),
        in_specs=[pl.BlockSpec(memory_space=pltpu.SMEM)] + [pl.BlockSpec(memory_space=pltpu.VMEM)] * (len(parts) + 1),
        out_shape=jax.ShapeDtypeStruct((count, TILE), jnp.float32),
        compiler_params=pltpu.CompilerParams(vmem_limit_bytes=VMEM),
        cost_estimate=pl.CostEstimate(flops=100_000_000, bytes_accessed=1_000_000, transcendentals=0),
        name="load",
    )(order, *parts, inverse)


def scatter_sum(turned, standard, gram):
    half = BLOCKS // 2 * TILE
    sent = totals(turned, standard, BLOCKS // 2, BLOCKS)
    got = exchange(sent, core_mask)
    got_gram = exchange(gram, core_mask)
    own = totals(turned, standard, 0, BLOCKS // 2)
    for mask in (first_mask, second_mask):
        half //= 2
        gram = gram + got_gram
        send = own[half:] + got[half:]
        own = own[:half] + got[:half]
        both = exchange(jnp.concatenate([send, gram], axis=0), mask)
        got, got_gram = both[:half], both[half:]
    gram = gram + got_gram
    own = own + got
    packets = []
    for q in range(1, 4):
        packet = jnp.concatenate([own[q * TILE : (q + 1) * TILE], gram], axis=0)
        packets.append(exchange(packet, lambda d, q=q: q << 3))
    total = jnp.concatenate([own[:TILE], gram], axis=0)
    total = (total + packets[0]) + (packets[1] + packets[2])
    bit = BLOCKS
    while bit < lax.axis_size(AXES):
        total = total + exchange(total, lambda d, bit=bit: bit)
        bit *= 2
    return total[:TILE], total[TILE:]


def along_z(own):
    return [own] + [exchange(own, lambda d, q=q: q << 3) for q in range(1, 4)]


def on_device(dosage, keep_rows, allele_counts, projection):
    groups = lax.axis_size(AXES)
    samples_total = dosage.shape[0] * groups
    kept_total = keep_rows.shape[0] * groups
    device = lax.axis_index("wide") * lax.axis_size("narrow") + lax.axis_index("narrow")
    order = block_order(device)
    keep = keep_rows.reshape(-1, TILE)
    counts = allele_counts.reshape(-1, TILE)
    standard, _, turned, gram, kept = standardize(samples_total, order, dosage, keep, counts, projection)
    own, gram = scatter_sum(turned, standard, gram)
    inverse = invert_factor(gram)
    near = jnp.concatenate(along_z(own), axis=0)
    plane = [near, exchange(near, second_mask)]
    plane = plane + [exchange(part, first_mask) for part in plane]
    parts = plane + [exchange(part, core_mask) for part in plane]
    projected, turned, gram = project(parts, inverse, standard, kept)
    own, gram = scatter_sum(turned, standard, gram)
    inverse = invert_factor(gram)
    near = jnp.concatenate(along_z(own), axis=0)
    parts = [near, exchange(near, lambda d: 4)]
    scores = score(math.sqrt(kept_total), keep, projected, inverse)
    position = lax.iota(jnp.int32, 8)
    place = (lax.axis_index("wide") & 7) ^ (((position & 3) << 1) | (position >> 2))
    loadings = load(place, parts, inverse)
    return (scores, loadings)


def solution(mesh):
    in_specs = (P(AXES, None), P(AXES), P(), P())
    out_specs = (P(AXES, None), P("narrow", None))
    return jax.shard_map(
        on_device, mesh=mesh, in_specs=in_specs, out_specs=out_specs, check_vma=False
    )
```

```python
import functools
import math

import jax
import jax.numpy as jnp
from jax import lax
from jax.experimental import pallas as pl
from jax.experimental.pallas import tpu as pltpu
from jax.sharding import PartitionSpec as P

AXES = ("wide", "narrow")
TILE = 128
BLOCKS = 32
ROWS = 256
VMEM = 28 * 1024 * 1024
SMALL = 16 * 1024 * 1024
GROUPS = 8


def split(value):
    high = value.astype(jnp.bfloat16)
    low = (value - high.astype(jnp.float32)).astype(jnp.bfloat16)
    return high, low


def product(left, right_high, right_low):
    high, low = split(left)
    dims = (((1,), (1,)), ((), ()))
    dot = functools.partial(lax.dot_general, dimension_numbers=dims, preferred_element_type=jnp.float32)
    return dot(high, right_high) + (dot(high, right_low) + dot(low, right_high))


def relative(position, core):
    first = (position >> 3) & 1
    second = (position >> 2) & 1
    core_bit = (position >> 4) & 1
    target = core ^ core_bit
    bit_x = jnp.where(target == 0, first, second)
    bit_y = jnp.where(target == 0, second, first)
    return core_bit | (bit_y << 1) | (bit_x << 2) | ((position & 3) << 3)


def block_order(device):
    position = lax.iota(jnp.int32, BLOCKS)
    owner = device ^ relative(position, device & 1)
    return (owner & 3) * 8 + ((owner >> 2) & 7)


def exchange(value, mask_of):
    count = lax.axis_size(AXES)
    return lax.ppermute(value, AXES, [(d, d ^ mask_of(d)) for d in range(count)])


def core_mask(d):
    return 1


def first_mask(d):
    return 2 if d & 1 else 4


def second_mask(d):
    return 4 if d & 1 else 2


def group_order(device):
    place = lax.iota(jnp.int32, GROUPS)
    return (((place >> 2) ^ (device & 1)) << 2) | ((place & 3) ^ ((device >> 3) & 3))


def standard_kernel(samples_total, order, dosage, keep, counts, projection, standard, projected, turned, gram, kept, rows_in, sketch_in, keep_in, counts_in, table, basis, whole, sems):
    samples = dosage.shape[0]
    steps = samples // ROWS
    small = [
        pltpu.make_async_copy(source, target, sems.at[i])
        for i, (source, target) in enumerate(((counts, counts_in), (keep, keep_in), (projection, sketch_in)))
    ]
    slabs = [slice(i * ROWS, (i + 1) * ROWS) for i in range(steps)]
    large = [
        pltpu.make_async_copy(dosage.at[slab, :], rows_in.at[slab, :], sems.at[3 + i]) for i, slab in enumerate(slabs)
    ]
    small[0].start()
    small[1].start()
    large[0].start()
    small[2].start()
    for copy in large[1:]:
        copy.start()
    small[0].wait()
    small[1].wait()
    frequency = counts_in[...].astype(jnp.float32) / (2.0 * samples_total)
    table[0] = 2.0 * frequency
    table[1] = 1.0 / jnp.sqrt(2.0 * frequency * (1.0 - frequency))
    for i in range(samples // TILE):
        rows = lax.broadcasted_iota(jnp.int32, (TILE, TILE), 0) + i * TILE
        found = jnp.zeros((TILE, TILE), jnp.float32)
        for j in range(keep.shape[0]):
            found = jnp.where(rows == keep_in[j : j + 1, :], 1.0, found)
        kept[i * TILE : (i + 1) * TILE, :] = jnp.broadcast_to(jnp.max(found, axis=1, keepdims=True), (TILE, TILE))
    for i, slab in enumerate(slabs):
        large[i].wait()
        if i == 0:
            small[2].wait()
            for p in range(BLOCKS):
                start = pl.multiple_of(order[p] * TILE, TILE)
                basis[p * TILE : (p + 1) * TILE, :] = sketch_in[pl.ds(start, TILE), :]
        for p in range(BLOCKS):
            block = order[p]
            center = table[0, pl.ds(block, 1), :]
            scale = table[1, pl.ds(block, 1), :]
            value = rows_in[slab, pl.ds(pl.multiple_of(block * TILE, TILE), TILE)].astype(jnp.float32)
            standard[slab, p * TILE : (p + 1) * TILE] = ((value - center) * scale).astype(jnp.bfloat16)
    project_rows(standard, basis, kept, projected, turned, whole)
    height = TILE // GROUPS
    for place in range(GROUPS):
        start = pl.multiple_of(order[BLOCKS + place] * height, height)
        gram[place * height : (place + 1) * height, :] = whole[pl.ds(start, height), :]


def project_rows(standard, basis, kept, projected, turned, gram):
    value = jnp.dot(standard[...], basis[...], preferred_element_type=jnp.float32)
    value = jnp.where(kept[...] > 0.0, value, 0.0)
    low = value.astype(jnp.bfloat16)
    low_turned = value.T.astype(jnp.bfloat16)
    projected[...] = low
    turned[...] = low_turned
    gram[...] = jnp.dot(low_turned, low, preferred_element_type=jnp.float32)


ON_CHIP = pl.BlockSpec(memory_space=pltpu.VMEM)
SCALARS = pl.BlockSpec(memory_space=pltpu.SMEM)
FAR = pl.BlockSpec(memory_space=pltpu.HBM)


def standardize(samples_total, order, *arrays):
    dosage, keep, counts, projection = [pltpu.with_memory_space_constraint(x, pltpu.HBM) for x in arrays]
    samples, snps = arrays[0].shape
    return pl.pallas_call(
        functools.partial(standard_kernel, samples_total),
        in_specs=[SCALARS, FAR, FAR, FAR, FAR],
        out_specs=[ON_CHIP] * 5,
        out_shape=[
            jax.ShapeDtypeStruct((samples, snps), jnp.bfloat16),
            jax.ShapeDtypeStruct((samples, TILE), jnp.bfloat16),
            jax.ShapeDtypeStruct((TILE, samples), jnp.bfloat16),
            jax.ShapeDtypeStruct((TILE, TILE), jnp.float32),
            jax.ShapeDtypeStruct((samples, TILE), jnp.float32),
        ],
        scratch_shapes=[
            pltpu.VMEM((samples, snps), jnp.bfloat16),
            pltpu.VMEM(arrays[3].shape, jnp.bfloat16),
            pltpu.VMEM(arrays[1].shape, jnp.int32),
            pltpu.VMEM(arrays[2].shape, jnp.int32),
            pltpu.VMEM((2,) + arrays[2].shape, jnp.float32),
            pltpu.VMEM(arrays[3].shape, jnp.bfloat16),
            pltpu.VMEM((TILE, TILE), jnp.float32),
            pltpu.SemaphoreType.DMA((3 + samples // ROWS,)),
        ],
        compiler_params=pltpu.CompilerParams(vmem_limit_bytes=VMEM),
        cost_estimate=pl.CostEstimate(flops=2 * samples * snps * TILE, bytes_accessed=4 * samples * snps, transcendentals=0),
        name="standardize",
    )(order, dosage, keep, counts, projection)


WIDTH = 512


def totals_kernel(low, high, turned, standard, *refs):
    out = refs[-1]
    base = low * TILE
    for start in range(base, high * TILE, WIDTH):
        value = jnp.dot(turned[...], standard[:, start : start + WIDTH], preferred_element_type=jnp.float32)
        out[start - base : start - base + WIDTH, :] = value.T
    if len(refs) == 2:
        tail = refs[0].shape[0] // 2
        out[(high - low) * TILE :, :] = refs[0][tail:, :]


def totals(turned, standard, low, high, *gram):
    samples = standard.shape[0]
    count = (high - low) * TILE
    tail = TILE // 2 if gram else 0
    return pl.pallas_call(
        functools.partial(totals_kernel, low, high),
        in_specs=[ON_CHIP] * (2 + len(gram)),
        out_specs=ON_CHIP,
        out_shape=jax.ShapeDtypeStruct((count + tail, TILE), jnp.float32),
        compiler_params=pltpu.CompilerParams(vmem_limit_bytes=SMALL),
        cost_estimate=pl.CostEstimate(flops=2 * samples * count * TILE, bytes_accessed=2 * samples * count, transcendentals=0),
        name="totals",
    )(turned, standard, *gram)


def combine_kernel(plan, count, *refs):
    for out, pieces in zip(refs[count:], plan):
        row = 0
        for rows, terms in pieces:
            values = [refs[index][start : start + rows, :] for index, start in terms]
            while len(values) > 1:
                values = [sum(values[i + 1 : i + 2], values[i]) for i in range(0, len(values), 2)]
            out[row : row + rows, :] = values[0]
            row += rows


def combine(arrays, plan):
    shapes = [jax.ShapeDtypeStruct((sum(rows for rows, _ in pieces), TILE), jnp.float32) for pieces in plan]
    size = sum(shape.shape[0] for shape in shapes) * TILE
    return pl.pallas_call(
        functools.partial(combine_kernel, plan, len(arrays)),
        in_specs=[ON_CHIP] * len(arrays),
        out_specs=[ON_CHIP] * len(plan),
        out_shape=shapes,
        compiler_params=pltpu.CompilerParams(vmem_limit_bytes=SMALL),
        cost_estimate=pl.CostEstimate(flops=2 * size, bytes_accessed=12 * size, transcendentals=0),
        name="combine",
    )(*arrays)


def project_kernel(pieces, *refs):
    parts = refs[:pieces]
    inverse, order, standard, kept, projected, turned, gram, basis, whole = refs[pieces:]
    high, low = split(inverse[...])
    start = 0
    for part in parts:
        size = part.shape[0]
        basis[start : start + size, :] = product(part[...], high, low).astype(jnp.bfloat16)
        start += size
    project_rows(standard, basis, kept, projected, turned, whole)
    height = TILE // GROUPS
    for place in range(GROUPS):
        start = pl.multiple_of(order[BLOCKS + place] * height, height)
        gram[place * height : (place + 1) * height, :] = whole[pl.ds(start, height), :]


def project(parts, inverse, order, standard, kept):
    samples, snps = standard.shape
    return pl.pallas_call(
        functools.partial(project_kernel, len(parts)),
        in_specs=[ON_CHIP] * (len(parts) + 1) + [SCALARS, ON_CHIP, ON_CHIP],
        out_specs=[ON_CHIP] * 3,
        out_shape=[
            jax.ShapeDtypeStruct((samples, TILE), jnp.bfloat16),
            jax.ShapeDtypeStruct((TILE, samples), jnp.bfloat16),
            jax.ShapeDtypeStruct((TILE, TILE), jnp.float32),
        ],
        scratch_shapes=[pltpu.VMEM((snps, TILE), jnp.bfloat16), pltpu.VMEM((TILE, TILE), jnp.float32)],
        compiler_params=pltpu.CompilerParams(vmem_limit_bytes=SMALL),
        cost_estimate=pl.CostEstimate(flops=2 * samples * snps * TILE, bytes_accessed=2 * samples * snps, transcendentals=0),
        name="project",
    )(*parts, inverse, order, standard, kept)


PANEL = 16


def inverse_kernel(own, other, order, out, left, right):
    height = TILE // GROUPS
    for half, source in enumerate((own, other)):
        for row in range(GROUPS // 2):
            start = pl.multiple_of(order[BLOCKS + half * (GROUPS // 2) + row] * height, height)
            left[pl.ds(start, height), :] = source[row * height : (row + 1) * height, :]
    lanes = lax.broadcasted_iota(jnp.int32, (TILE, TILE), 1)
    subs = lax.broadcasted_iota(jnp.int32, (TILE, TILE), 0)
    right[...] = jnp.where(lanes == subs, 1.0, 0.0)
    panel_rows = lax.broadcasted_iota(jnp.int32, (PANEL, TILE), 0)
    for start in range(0, TILE, PANEL):
        stop = start + PANEL
        upper = left[start:stop, :]
        done = right[start:stop, :]
        columns = [
            jnp.broadcast_to(upper[:, start + j : start + j + 1], (PANEL, TILE)) for j in range(PANEL)
        ]
        for k in range(PANEL):
            pivot = columns[k][k : k + 1, :]
            root = lax.rsqrt(pivot)
            below = jnp.where(panel_rows > k, columns[k] * (root * root), 0.0)
            for j in range(k + 1, PANEL):
                columns[j] = columns[j] - below * columns[j][k : k + 1, :]
            factor = jnp.where(panel_rows == k, root, 1.0)
            upper = upper * factor - below * upper[k : k + 1, :]
            done = done * factor - below * done[k : k + 1, :]
        out[start:stop, :] = done
        if stop < TILE:
            both = lax.dot_general(
                upper,
                jnp.concatenate([upper, done], axis=1),
                (((0,), (0,)), ((), ())),
                precision=lax.Precision.HIGHEST,
                preferred_element_type=jnp.float32,
            )
            left[stop:, :] -= both[stop:, :TILE]
            right[stop:, :] -= both[stop:, TILE:]


def invert_factor(own, other, order):
    return pl.pallas_call(
        inverse_kernel,
        in_specs=[ON_CHIP, ON_CHIP, SCALARS],
        out_specs=ON_CHIP,
        out_shape=jax.ShapeDtypeStruct((TILE, TILE), jnp.float32),
        scratch_shapes=[pltpu.VMEM((TILE, TILE), jnp.float32), pltpu.VMEM((TILE, TILE), jnp.float32)],
        compiler_params=pltpu.CompilerParams(vmem_limit_bytes=SMALL),
        cost_estimate=pl.CostEstimate(flops=2_000_000_000, bytes_accessed=16_000_000, transcendentals=0),
        name="invert_factor",
    )(own, other, order)


def pick_kernel(keep, projected, chosen):
    samples = projected.shape[0]
    lanes = lax.broadcasted_iota(jnp.int32, (TILE, samples), 1).astype(jnp.float32)
    for j in range(keep.shape[0]):
        row = jnp.broadcast_to(keep[j : j + 1, :].astype(jnp.float32), (TILE, TILE)).T
        pick = jnp.where(lanes == jnp.tile(row, (1, samples // TILE)), 1.0, 0.0).astype(jnp.bfloat16)
        value = jnp.dot(pick, projected[...], preferred_element_type=jnp.float32)
        chosen[j * TILE : (j + 1) * TILE, :] = value.astype(jnp.bfloat16)


def pick_rows(keep, projected):
    return pl.pallas_call(
        pick_kernel,
        in_specs=[ON_CHIP, ON_CHIP],
        out_specs=ON_CHIP,
        out_shape=jax.ShapeDtypeStruct((keep.shape[0] * TILE, TILE), jnp.bfloat16),
        compiler_params=pltpu.CompilerParams(vmem_limit_bytes=SMALL),
        cost_estimate=pl.CostEstimate(flops=500_000_000, bytes_accessed=4_000_000, transcendentals=0),
        name="pick_rows",
    )(keep, projected)


def scores_kernel(scale, chosen, inverse, scores):
    high, low = split(inverse[...])
    dims = (((1,), (1,)), ((), ()))
    value = lax.dot_general(chosen[...], high, dims, preferred_element_type=jnp.float32)
    value = value + lax.dot_general(chosen[...], low, dims, preferred_element_type=jnp.float32)
    scores[...] = value * scale


def score(scale, chosen, inverse):
    return pl.pallas_call(
        functools.partial(scores_kernel, scale),
        out_shape=jax.ShapeDtypeStruct(chosen.shape, jnp.float32),
        compiler_params=pltpu.CompilerParams(vmem_limit_bytes=SMALL),
        cost_estimate=pl.CostEstimate(flops=500_000_000, bytes_accessed=4_000_000, transcendentals=0),
        name="score",
    )(chosen, inverse)


def loadings_kernel(pieces, order, *refs):
    parts = refs[:pieces]
    inverse, loadings = refs[pieces:]
    high, low = split(inverse[...])
    position = 0
    for part in parts:
        for row in range(0, part.shape[0], TILE):
            start = pl.multiple_of(order[position] * TILE, TILE)
            loadings[pl.ds(start, TILE), :] = product(part[row : row + TILE, :], high, low)
            position += 1


def load(order, parts, inverse):
    count = sum(part.shape[0] for part in parts)
    return pl.pallas_call(
        functools.partial(loadings_kernel, len(parts)),
        in_specs=[pl.BlockSpec(memory_space=pltpu.SMEM)] + [pl.BlockSpec(memory_space=pltpu.VMEM)] * (len(parts) + 1),
        out_shape=jax.ShapeDtypeStruct((count, TILE), jnp.float32),
        compiler_params=pltpu.CompilerParams(vmem_limit_bytes=VMEM),
        cost_estimate=pl.CostEstimate(flops=100_000_000, bytes_accessed=1_000_000, transcendentals=0),
        name="load",
    )(order, *parts, inverse)


def span(rows, *terms):
    return (rows, terms)


def scatter_sum(turned, standard, gram):
    four = 4 * TILE
    eight = 8 * TILE
    slot = TILE // GROUPS
    half = TILE // 2
    far = exchange(totals(turned, standard, 24, 32, gram), core_mask)
    close = exchange(totals(turned, standard, 16, 24), core_mask)
    own = totals(turned, standard, 0, 16)
    (send,) = combine(
        [own, far, gram],
        [[span(four, (0, eight + four), (1, four)), span(half, (2, 0), (1, eight))]],
    )
    first = exchange(send, first_mask)
    (send_rest,) = combine([own, far], [[span(four, (0, eight), (1, 0))]])
    rest = exchange(send_rest, first_mask)
    (send_next,) = combine(
        [own, close, first, send],
        [[span(four, (0, four), (1, four), (2, 0)), span(half, (3, four), (2, four))]],
    )
    second = exchange(send_next, second_mask)
    packets = combine(
        [own, close, rest, second, send_next],
        [
            [
                span(TILE, (0, q * TILE), (1, q * TILE), (2, q * TILE), (3, q * TILE)),
                span(slot, (4, four + q * slot), (3, four + q * slot)),
            ]
            for q in range(4)
        ],
    )
    return packets


def along_z(value):
    return [exchange(value, lambda d, q=q: q << 3) for q in range(1, 4)]


def finish_sum(packets):
    size = TILE + TILE // GROUPS
    arrived = [exchange(packets[q], lambda d, q=q: q << 3) for q in range(1, 4)]
    (total,) = combine([packets[0]] + arrived, [[span(size, *((q, 0) for q in range(4)))]])
    bit = BLOCKS
    while bit < lax.axis_size(AXES):
        total = total + exchange(total, lambda d, bit=bit: bit)
        bit *= 2
    return total


def gather_near(total):
    arrived = [total] + along_z(total)
    slot = TILE // GROUPS
    return combine(
        arrived,
        [[span(TILE, (q, 0)) for q in range(4)], [span(slot, (q, TILE)) for q in range(4)]],
    )


def on_device(dosage, keep_rows, allele_counts, projection):
    groups = lax.axis_size(AXES)
    samples_total = dosage.shape[0] * groups
    kept_total = keep_rows.shape[0] * groups
    device = lax.axis_index("wide") * lax.axis_size("narrow") + lax.axis_index("narrow")
    order = jnp.concatenate([block_order(device), group_order(device)])
    keep = keep_rows.reshape(-1, TILE)
    counts = allele_counts.reshape(-1, TILE)
    standard, _, turned, gram, kept = standardize(samples_total, order, dosage, keep, counts, projection)
    total = finish_sum(scatter_sum(turned, standard, gram))
    near, own_gram = gather_near(total)
    across = exchange(near, second_mask)
    along = exchange(near, first_mask)
    inverse = invert_factor(own_gram, exchange(own_gram, core_mask), order)
    across, inverse = lax.optimization_barrier((across, inverse))
    plane = [near, across, along, exchange(across, first_mask)]
    parts = plane + [exchange(part, core_mask) for part in plane]
    projected, turned, gram = project(parts, inverse, order, standard, kept)
    packets = scatter_sum(turned, standard, gram)
    total = finish_sum(packets)
    chosen = pick_rows(keep, projected)
    total, chosen = lax.optimization_barrier((total, chosen))
    near, own_gram = gather_near(total)
    parts = [near, exchange(near, lambda d: 4)]
    inverse = invert_factor(own_gram, exchange(own_gram, core_mask), order)
    scores = score(math.sqrt(kept_total), chosen, inverse)
    position = lax.iota(jnp.int32, 8)
    place = (lax.axis_index("wide") & 7) ^ (((position & 3) << 1) | (position >> 2))
    loadings = load(place, parts, inverse)
    return (scores, loadings)


def solution(mesh):
    in_specs = (P(AXES, None), P(AXES), P(), P())
    out_specs = (P(AXES, None), P("narrow", None))
    return jax.shard_map(
        on_device, mesh=mesh, in_specs=in_specs, out_specs=out_specs, check_vma=False
    )
```

```python
import functools
import math

import jax
import jax.numpy as jnp
from jax import lax
from jax.experimental import pallas as pl
from jax.experimental.pallas import tpu as pltpu
from jax.sharding import PartitionSpec as P

AXES = ("wide", "narrow")
TILE = 128
BLOCKS = 32
ROWS = 256
VMEM = 28 * 1024 * 1024
SMALL = 16 * 1024 * 1024
GROUPS = 8
HALF = TILE // 2


def split(value):
    high = value.astype(jnp.bfloat16)
    low = (value - high.astype(jnp.float32)).astype(jnp.bfloat16)
    return high, low


def thirds(value):
    high = value.astype(jnp.bfloat16)
    return (high,) + split(value - high.astype(jnp.float32))


def product(left, right_high, right_low):
    high, low = split(left)
    dims = (((1,), (1,)), ((), ()))
    dot = functools.partial(lax.dot_general, dimension_numbers=dims, preferred_element_type=jnp.float32)
    return dot(high, right_high) + (dot(high, right_low) + dot(low, right_high))


def relative(position, core):
    first = (position >> 3) & 1
    second = (position >> 2) & 1
    core_bit = (position >> 4) & 1
    target = core ^ core_bit
    bit_x = jnp.where(target == 0, first, second)
    bit_y = jnp.where(target == 0, second, first)
    return core_bit | (bit_y << 1) | (bit_x << 2) | ((position & 3) << 3)


def block_order(device):
    position = lax.iota(jnp.int32, BLOCKS)
    owner = device ^ relative(position, device & 1)
    return (owner & 3) * 8 + ((owner >> 2) & 7)


def exchange(value, mask_of):
    count = lax.axis_size(AXES)
    return lax.ppermute(value, AXES, [(d, d ^ mask_of(d)) for d in range(count)])


def core_mask(d):
    return 1


def first_mask(d):
    return 2 if d & 1 else 4


def second_mask(d):
    return 4 if d & 1 else 2


def group_order(device):
    place = lax.iota(jnp.int32, GROUPS)
    return (((place >> 2) ^ (device & 1)) << 2) | ((place & 3) ^ ((device >> 3) & 3))


def standard_kernel(samples_total, order, dosage, keep, counts, projection, standard, projected, turned, gram, kept, rows_in, sketch_in, keep_in, counts_in, table, basis, whole, sems):
    samples = dosage.shape[0]
    steps = samples // ROWS
    small = [
        pltpu.make_async_copy(source, target, sems.at[i])
        for i, (source, target) in enumerate(((counts, counts_in), (keep, keep_in), (projection, sketch_in)))
    ]
    slabs = [slice(i * ROWS, (i + 1) * ROWS) for i in range(steps)]
    large = [
        pltpu.make_async_copy(dosage.at[slab, :], rows_in.at[slab, :], sems.at[3 + i]) for i, slab in enumerate(slabs)
    ]
    small[0].start()
    small[1].start()
    large[0].start()
    small[2].start()
    for copy in large[1:]:
        copy.start()
    small[0].wait()
    small[1].wait()
    frequency = counts_in[...].astype(jnp.float32) / (2.0 * samples_total)
    table[0] = 2.0 * frequency
    table[1] = 1.0 / jnp.sqrt(2.0 * frequency * (1.0 - frequency))
    for i in range(samples // TILE):
        rows = lax.broadcasted_iota(jnp.int32, (TILE, TILE), 0) + i * TILE
        found = jnp.zeros((TILE, TILE), jnp.float32)
        for j in range(keep.shape[0]):
            found = jnp.where(rows == keep_in[j : j + 1, :], 1.0, found)
        kept[i * TILE : (i + 1) * TILE, :] = jnp.broadcast_to(jnp.max(found, axis=1, keepdims=True), (TILE, TILE))
    for i, slab in enumerate(slabs):
        large[i].wait()
        if i == 0:
            small[2].wait()
            for p in range(BLOCKS):
                start = pl.multiple_of(order[p] * TILE, TILE)
                basis[p * TILE : (p + 1) * TILE, :] = sketch_in[pl.ds(start, TILE), :]
        for p in range(BLOCKS):
            block = order[p]
            center = table[0, pl.ds(block, 1), :]
            scale = table[1, pl.ds(block, 1), :]
            value = rows_in[slab, pl.ds(pl.multiple_of(block * TILE, TILE), TILE)].astype(jnp.float32)
            standard[slab, p * TILE : (p + 1) * TILE] = ((value - center) * scale).astype(jnp.bfloat16)
    value = jnp.dot(standard[...], basis[...], preferred_element_type=jnp.float32)
    finish_rows(value, kept, projected, turned, whole)
    share_gram(order, whole, gram)


def share_gram(order, whole, gram):
    height = TILE // GROUPS
    for place in range(GROUPS):
        start = pl.multiple_of(order[BLOCKS + place] * height, height)
        gram[place * height : (place + 1) * height, :] = whole[pl.ds(start, height), :]


def finish_rows(value, kept, projected, turned, gram):
    value = jnp.where(kept[...] > 0.0, value, 0.0)
    low = value.astype(jnp.bfloat16)
    low_turned = value.T.astype(jnp.bfloat16)
    projected[...] = low
    turned[...] = low_turned
    gram[...] = jnp.dot(low_turned, low, preferred_element_type=jnp.float32)


ON_CHIP = pl.BlockSpec(memory_space=pltpu.VMEM)
SCALARS = pl.BlockSpec(memory_space=pltpu.SMEM)
FAR = pl.BlockSpec(memory_space=pltpu.HBM)


def standardize(samples_total, order, *arrays):
    dosage, keep, counts, projection = [pltpu.with_memory_space_constraint(x, pltpu.HBM) for x in arrays]
    samples, snps = arrays[0].shape
    return pl.pallas_call(
        functools.partial(standard_kernel, samples_total),
        in_specs=[SCALARS, FAR, FAR, FAR, FAR],
        out_specs=[ON_CHIP] * 5,
        out_shape=[
            jax.ShapeDtypeStruct((samples, snps), jnp.bfloat16),
            jax.ShapeDtypeStruct((samples, TILE), jnp.bfloat16),
            jax.ShapeDtypeStruct((TILE, samples), jnp.bfloat16),
            jax.ShapeDtypeStruct((TILE, TILE), jnp.float32),
            jax.ShapeDtypeStruct((samples, TILE), jnp.float32),
        ],
        scratch_shapes=[
            pltpu.VMEM((samples, snps), jnp.bfloat16),
            pltpu.VMEM(arrays[3].shape, jnp.bfloat16),
            pltpu.VMEM(arrays[1].shape, jnp.int32),
            pltpu.VMEM(arrays[2].shape, jnp.int32),
            pltpu.VMEM((2,) + arrays[2].shape, jnp.float32),
            pltpu.VMEM(arrays[3].shape, jnp.bfloat16),
            pltpu.VMEM((TILE, TILE), jnp.float32),
            pltpu.SemaphoreType.DMA((3 + samples // ROWS,)),
        ],
        compiler_params=pltpu.CompilerParams(vmem_limit_bytes=VMEM),
        cost_estimate=pl.CostEstimate(flops=2 * samples * snps * TILE, bytes_accessed=4 * samples * snps, transcendentals=0),
        name="standardize",
    )(order, dosage, keep, counts, projection)


WIDTH = 512


def totals_kernel(low, high, turned, standard, *refs):
    out = refs[-1]
    base = low * TILE
    for start in range(base, high * TILE, WIDTH):
        value = jnp.dot(turned[...], standard[:, start : start + WIDTH], preferred_element_type=jnp.float32)
        out[start - base : start - base + WIDTH, :] = value.T
    if len(refs) == 2:
        tail = refs[0].shape[0] // 2
        out[(high - low) * TILE :, :] = refs[0][tail:, :]


def totals(turned, standard, low, high, *gram):
    samples = standard.shape[0]
    count = (high - low) * TILE
    tail = TILE // 2 if gram else 0
    return pl.pallas_call(
        functools.partial(totals_kernel, low, high),
        in_specs=[ON_CHIP] * (2 + len(gram)),
        out_specs=ON_CHIP,
        out_shape=jax.ShapeDtypeStruct((count + tail, TILE), jnp.float32),
        compiler_params=pltpu.CompilerParams(vmem_limit_bytes=SMALL),
        cost_estimate=pl.CostEstimate(flops=2 * samples * count * TILE, bytes_accessed=2 * samples * count, transcendentals=0),
        name="totals",
    )(turned, standard, *gram)


def combine_kernel(plan, count, *refs):
    for out, pieces in zip(refs[count:], plan):
        row = 0
        for rows, terms in pieces:
            values = [refs[index][start : start + rows, :] for index, start in terms]
            while len(values) > 1:
                values = [sum(values[i + 1 : i + 2], values[i]) for i in range(0, len(values), 2)]
            out[row : row + rows, :] = values[0]
            row += rows


def combine(arrays, plan):
    shapes = [jax.ShapeDtypeStruct((sum(rows for rows, _ in pieces), TILE), jnp.float32) for pieces in plan]
    size = sum(shape.shape[0] for shape in shapes) * TILE
    return pl.pallas_call(
        functools.partial(combine_kernel, plan, len(arrays)),
        in_specs=[ON_CHIP] * len(arrays),
        out_specs=[ON_CHIP] * len(plan),
        out_shape=shapes,
        compiler_params=pltpu.CompilerParams(vmem_limit_bytes=SMALL),
        cost_estimate=pl.CostEstimate(flops=2 * size, bytes_accessed=12 * size, transcendentals=0),
        name="combine",
    )(*arrays)


def apply_inverse(parts, inverse, basis):
    high, low = split(inverse[...])
    start = 0
    for part in parts:
        size = part.shape[0]
        basis[start : start + size, :] = product(part[...], high, low).astype(jnp.bfloat16)
        start += size


def add_products(standard, basis, base, value):
    row = 0
    for first, count in base:
        size = count * TILE
        term = jnp.dot(
            standard[:, first * TILE : first * TILE + size],
            basis[row : row + size, :],
            preferred_element_type=jnp.float32,
        )
        value = term if value is None else value + term
        row += size
    return value


def begin_kernel(pieces, base, *refs):
    parts = refs[:pieces]
    inverse, standard, out, basis = refs[pieces:]
    apply_inverse(parts, inverse, basis)
    out[...] = add_products(standard, basis, base, None)


def begin_project(parts, base, inverse, standard):
    samples = standard.shape[0]
    rows = sum(part.shape[0] for part in parts)
    return pl.pallas_call(
        functools.partial(begin_kernel, len(parts), base),
        in_specs=[ON_CHIP] * (len(parts) + 2),
        out_specs=ON_CHIP,
        out_shape=jax.ShapeDtypeStruct((samples, TILE), jnp.float32),
        scratch_shapes=[pltpu.VMEM((rows, TILE), jnp.bfloat16)],
        compiler_params=pltpu.CompilerParams(vmem_limit_bytes=SMALL),
        cost_estimate=pl.CostEstimate(flops=2 * samples * rows * TILE, bytes_accessed=2 * samples * rows, transcendentals=0),
        name="begin_project",
    )(*parts, inverse, standard)


def project_kernel(pieces, base, *refs):
    parts = refs[:pieces]
    begun, inverse, order, standard, kept, projected, turned, gram, basis, whole = refs[pieces:]
    apply_inverse(parts, inverse, basis)
    value = add_products(standard, basis, base, begun[...])
    finish_rows(value, kept, projected, turned, whole)
    share_gram(order, whole, gram)


def project(parts, base, begun, inverse, order, standard, kept):
    samples = standard.shape[0]
    rows = sum(part.shape[0] for part in parts)
    return pl.pallas_call(
        functools.partial(project_kernel, len(parts), base),
        in_specs=[ON_CHIP] * (len(parts) + 2) + [SCALARS, ON_CHIP, ON_CHIP],
        out_specs=[ON_CHIP] * 3,
        out_shape=[
            jax.ShapeDtypeStruct((samples, TILE), jnp.bfloat16),
            jax.ShapeDtypeStruct((TILE, samples), jnp.bfloat16),
            jax.ShapeDtypeStruct((TILE, TILE), jnp.float32),
        ],
        scratch_shapes=[pltpu.VMEM((rows, TILE), jnp.bfloat16), pltpu.VMEM((TILE, TILE), jnp.float32)],
        compiler_params=pltpu.CompilerParams(vmem_limit_bytes=SMALL),
        cost_estimate=pl.CostEstimate(flops=2 * samples * rows * TILE, bytes_accessed=2 * samples * rows, transcendentals=0),
        name="project",
    )(*parts, begun, inverse, order, standard, kept)


PANEL = 16


def eliminate(first, last, left, right, out):
    panel_rows = lax.broadcasted_iota(jnp.int32, (PANEL, TILE), 0)
    for start in range(first, last, PANEL):
        stop = start + PANEL
        upper = left[start:stop, :]
        done = right[start:stop, :]
        columns = [
            jnp.broadcast_to(upper[:, start + j : start + j + 1], (PANEL, TILE)) for j in range(PANEL)
        ]
        for k in range(PANEL):
            pivot = columns[k][k : k + 1, :]
            root = lax.rsqrt(pivot)
            below = jnp.where(panel_rows > k, columns[k] * (root * root), 0.0)
            for j in range(k + 1, PANEL):
                columns[j] = columns[j] - below * columns[j][k : k + 1, :]
            factor = jnp.where(panel_rows == k, root, 1.0)
            upper = upper * factor - below * upper[k : k + 1, :]
            done = done * factor - below * done[k : k + 1, :]
        out[start:stop, :] = done
        if stop < TILE:
            left_parts = thirds(upper)
            right_parts = thirds(jnp.concatenate([upper, done], axis=1))
            pairs = ((0, 0), (0, 1), (1, 0), (0, 2), (1, 1), (2, 0))
            both = lax.dot_general(
                jnp.concatenate([left_parts[i] for i, _ in pairs], axis=0),
                jnp.concatenate([right_parts[j] for _, j in pairs], axis=0),
                (((0,), (0,)), ((), ())),
                preferred_element_type=jnp.float32,
            )
            left[stop:, :] -= both[stop:, :TILE]
            right[stop:, :] -= both[stop:, TILE:]


def begin_kernel_inverse(last, own, other, order, left, right):
    height = TILE // GROUPS
    for half, source in enumerate((own, other)):
        for row in range(GROUPS // 2):
            start = pl.multiple_of(order[BLOCKS + half * (GROUPS // 2) + row] * height, height)
            left[pl.ds(start, height), :] = source[row * height : (row + 1) * height, :]
    lanes = lax.broadcasted_iota(jnp.int32, (TILE, TILE), 1)
    subs = lax.broadcasted_iota(jnp.int32, (TILE, TILE), 0)
    right[...] = jnp.where(lanes == subs, 1.0, 0.0)
    eliminate(0, last, left, right, right)


def end_kernel_inverse(first, left_in, right_in, out, left, right):
    left[first:, :] = left_in[first:, :]
    right[first:, :] = right_in[first:, :]
    out[:first, :] = right_in[:first, :]
    eliminate(first, TILE, left, right, out)


SQUARE = jax.ShapeDtypeStruct((TILE, TILE), jnp.float32)


def begin_inverse(last, own, other, order):
    return pl.pallas_call(
        functools.partial(begin_kernel_inverse, last),
        in_specs=[ON_CHIP, ON_CHIP, SCALARS],
        out_specs=[ON_CHIP, ON_CHIP],
        out_shape=[SQUARE, SQUARE],
        compiler_params=pltpu.CompilerParams(vmem_limit_bytes=SMALL),
        cost_estimate=pl.CostEstimate(flops=1_000_000_000, bytes_accessed=8_000_000, transcendentals=0),
        name="begin_inverse",
    )(own, other, order)


def end_inverse(first, left, right):
    return pl.pallas_call(
        functools.partial(end_kernel_inverse, first),
        in_specs=[ON_CHIP, ON_CHIP],
        out_specs=ON_CHIP,
        out_shape=SQUARE,
        scratch_shapes=[pltpu.VMEM((TILE, TILE), jnp.float32), pltpu.VMEM((TILE, TILE), jnp.float32)],
        compiler_params=pltpu.CompilerParams(vmem_limit_bytes=SMALL),
        cost_estimate=pl.CostEstimate(flops=1_000_000_000, bytes_accessed=8_000_000, transcendentals=0),
        name="end_inverse",
    )(left, right)


def invert_factor(own, other, order):
    return begin_inverse(TILE, own, other, order)[1]


def pick_kernel(keep, projected, chosen):
    samples = projected.shape[0]
    lanes = lax.broadcasted_iota(jnp.int32, (TILE, samples), 1).astype(jnp.float32)
    for j in range(keep.shape[0]):
        row = jnp.broadcast_to(keep[j : j + 1, :].astype(jnp.float32), (TILE, TILE)).T
        pick = jnp.where(lanes == jnp.tile(row, (1, samples // TILE)), 1.0, 0.0).astype(jnp.bfloat16)
        value = jnp.dot(pick, projected[...], preferred_element_type=jnp.float32)
        chosen[j * TILE : (j + 1) * TILE, :] = value.astype(jnp.bfloat16)


def pick_rows(keep, projected):
    return pl.pallas_call(
        pick_kernel,
        in_specs=[ON_CHIP, ON_CHIP],
        out_specs=ON_CHIP,
        out_shape=jax.ShapeDtypeStruct((keep.shape[0] * TILE, TILE), jnp.bfloat16),
        compiler_params=pltpu.CompilerParams(vmem_limit_bytes=SMALL),
        cost_estimate=pl.CostEstimate(flops=500_000_000, bytes_accessed=4_000_000, transcendentals=0),
        name="pick_rows",
    )(keep, projected)


def scores_kernel(scale, chosen, inverse, scores):
    high, low = split(inverse[...])
    dims = (((1,), (1,)), ((), ()))
    value = lax.dot_general(chosen[...], high, dims, preferred_element_type=jnp.float32)
    value = value + lax.dot_general(chosen[...], low, dims, preferred_element_type=jnp.float32)
    scores[...] = value * scale


def score(scale, chosen, inverse):
    return pl.pallas_call(
        functools.partial(scores_kernel, scale),
        out_shape=jax.ShapeDtypeStruct(chosen.shape, jnp.float32),
        compiler_params=pltpu.CompilerParams(vmem_limit_bytes=SMALL),
        cost_estimate=pl.CostEstimate(flops=500_000_000, bytes_accessed=4_000_000, transcendentals=0),
        name="score",
    )(chosen, inverse)


def loadings_kernel(pieces, order, *refs):
    parts = refs[:pieces]
    inverse, loadings = refs[pieces:]
    high, low = split(inverse[...])
    value = product(jnp.concatenate([part[...] for part in parts], axis=0), high, low)
    for position in range(value.shape[0] // TILE):
        start = pl.multiple_of(order[position] * TILE, TILE)
        loadings[pl.ds(start, TILE), :] = value[position * TILE : (position + 1) * TILE, :]


def load(order, parts, inverse):
    count = sum(part.shape[0] for part in parts)
    return pl.pallas_call(
        functools.partial(loadings_kernel, len(parts)),
        in_specs=[pl.BlockSpec(memory_space=pltpu.SMEM)] + [pl.BlockSpec(memory_space=pltpu.VMEM)] * (len(parts) + 1),
        out_shape=jax.ShapeDtypeStruct((count, TILE), jnp.float32),
        compiler_params=pltpu.CompilerParams(vmem_limit_bytes=VMEM),
        cost_estimate=pl.CostEstimate(flops=100_000_000, bytes_accessed=1_000_000, transcendentals=0),
        name="load",
    )(order, *parts, inverse)


def span(rows, *terms):
    return (rows, terms)


def scatter_sum(turned, standard, gram):
    four = 4 * TILE
    eight = 8 * TILE
    slot = TILE // GROUPS
    half = TILE // 2
    three = 3 * TILE
    far = exchange(totals(turned, standard, 24, 32, gram), core_mask)
    upper = totals(turned, standard, 8, 16)
    send, send_rest = combine(
        [upper, far, gram],
        [
            [span(three, (0, four + TILE), (1, four + TILE)), span(half, (2, 0), (1, eight))],
            [span(four + TILE, (0, 0), (1, 0))],
        ],
    )
    first = exchange(send, first_mask)
    rest = exchange(send_rest, first_mask)
    close = exchange(totals(turned, standard, 16, 24), core_mask)
    own = totals(turned, standard, 0, 8)
    (send_next,) = combine(
        [own, close, first, send],
        [[span(three, (0, four + TILE), (1, four + TILE), (2, 0)), span(half, (3, three), (2, three))]],
    )
    second = exchange(send_next, second_mask)
    (send_last,) = combine([own, close, rest], [[span(TILE, (0, four), (1, four), (2, four))]])
    last = exchange(send_last, second_mask)

    def share(q):
        return span(slot, (4, three + q * slot), (3, three + q * slot))

    def packet(q):
        start = q * TILE
        return [span(TILE, (0, start), (1, start), (2, start), (3, start - TILE)), share(q)]

    *packets, own_share = combine(
        [own, close, rest, second, send_next], [packet(q) for q in (3, 2, 1)] + [[share(0)]]
    )
    arrived = [exchange(packet, lambda d, q=q: (3 - q) << 3) for q, packet in enumerate(packets)]
    total, share = combine(
        [own, close, rest, last, own_share] + arrived,
        [
            [span(TILE, *((i, 0) for i in (0, 1, 2, 3, 5, 6, 7)))],
            [span(slot, (4, 0), (7, TILE), (6, TILE), (5, TILE))],
        ],
    )
    return across_rest(total), across_rest(share)


def across_rest(value):
    bit = BLOCKS
    while bit < lax.axis_size(AXES):
        value = value + exchange(value, lambda d, bit=bit: bit)
        bit *= 2
    return value


def along_z(value):
    return [exchange(value, lambda d, q=q: q << 3) for q in range(1, 4)]


def gather_near(total, share):
    slot = TILE // GROUPS
    (packet,) = combine([total, share], [[span(TILE, (0, 0)), span(slot, (1, 0))]])
    return combine(
        [packet] + along_z(packet),
        [[span(TILE, (q, 0)) for q in range(4)], [span(slot, (q, TILE)) for q in range(4)]],
    )


def gather_last(total, share, mask):
    slot = TILE // GROUPS
    (packet,) = combine([total, share], [[span(TILE, (0, 0)), span(slot, (1, 0))]])
    arrived = along_z(packet)
    return combine(
        [total, share] + arrived + [exchange(total, mask)],
        [
            [span(TILE, (i, 0)) for i in (2, 3, 4)],
            [span(slot, (1, 0))] + [span(slot, (i, TILE)) for i in (2, 3, 4)],
            [span(TILE, (0, 0)), span(TILE, (5, 0))],
        ],
    )


def on_device(dosage, keep_rows, allele_counts, projection):
    groups = lax.axis_size(AXES)
    samples_total = dosage.shape[0] * groups
    kept_total = keep_rows.shape[0] * groups
    device = lax.axis_index("wide") * lax.axis_size("narrow") + lax.axis_index("narrow")
    order = jnp.concatenate([block_order(device), group_order(device)])
    keep = keep_rows.reshape(-1, TILE)
    counts = allele_counts.reshape(-1, TILE)
    standard, _, turned, gram, kept = standardize(samples_total, order, dosage, keep, counts, projection)
    total, share = scatter_sum(turned, standard, gram)
    near, share = gather_near(total, share)
    across = exchange(near, second_mask)
    other = exchange(share, core_mask)
    later, other = lax.optimization_barrier((near, other))
    along = exchange(later, first_mask)
    middle = begin_inverse(HALF, share, other, order)
    across, middle = lax.optimization_barrier((across, middle))
    corner = exchange(across, first_mask)
    inverse = end_inverse(HALF, *middle)
    early = [near, across, along] + [exchange(part, core_mask) for part in (near, across)]
    begun = begin_project(early, [(0, 4), (4, 4), (8, 4), (16, 4), (20, 4)], inverse, standard)
    corner, begun = lax.optimization_barrier((corner, begun))
    late = [exchange(along, core_mask), corner, exchange(corner, core_mask)]
    ranges = [(24, 4), (12, 4), (28, 4)]
    projected, turned, gram = project(late, ranges, begun, inverse, order, standard, kept)
    total, share = scatter_sum(turned, standard, gram)
    chosen = pick_rows(keep, projected)
    total, chosen = lax.optimization_barrier((total, chosen))
    near, share, corners = gather_last(total, share, lambda d: 4)
    beside = exchange(near, lambda d: 4)
    inverse = invert_factor(share, exchange(share, core_mask), order)
    scores = score(math.sqrt(kept_total), chosen, inverse)
    position = jnp.array([0, 4, 1, 2, 3, 5, 6, 7], jnp.int32)
    place = (lax.axis_index("wide") & 7) ^ (((position & 3) << 1) | (position >> 2))
    loadings = load(place, [corners, near, beside], inverse)
    return (scores, loadings)


def solution(mesh):
    in_specs = (P(AXES, None), P(AXES), P(), P())
    out_specs = (P(AXES, None), P("narrow", None))
    return jax.shard_map(
        on_device, mesh=mesh, in_specs=in_specs, out_specs=out_specs, check_vma=False
    )
```

```python
import functools
import math

import jax
import jax.numpy as jnp
from jax import lax
from jax.experimental import pallas as pl
from jax.experimental.pallas import tpu as pltpu
from jax.sharding import PartitionSpec as P

AXES = ("wide", "narrow")
TILE = 128
BLOCKS = 32
ROWS = 256
VMEM = 28 * 1024 * 1024
SMALL = 16 * 1024 * 1024
GROUPS = 8
HALF = TILE // 2


def split(value):
    high = value.astype(jnp.bfloat16)
    low = (value - high.astype(jnp.float32)).astype(jnp.bfloat16)
    return high, low


def thirds(value):
    high = value.astype(jnp.bfloat16)
    return (high,) + split(value - high.astype(jnp.float32))


def product(left, right_high, right_low):
    high, low = split(left)
    dims = (((1,), (1,)), ((), ()))
    dot = functools.partial(lax.dot_general, dimension_numbers=dims, preferred_element_type=jnp.float32)
    return dot(high, right_high) + (dot(high, right_low) + dot(low, right_high))


def relative(position, core):
    first = (position >> 3) & 1
    second = (position >> 2) & 1
    core_bit = (position >> 4) & 1
    target = core ^ core_bit
    bit_x = first * (1 - target) + second * target
    bit_y = second * (1 - target) + first * target
    return core_bit | (bit_y << 1) | (bit_x << 2) | ((position & 3) << 3)


def this_device():
    return lax.axis_index("wide") * lax.axis_size("narrow") + lax.axis_index("narrow")


def block_at(device, position):
    owner = device ^ relative(position, device & 1)
    return (owner & 3) * 8 + ((owner >> 2) & 7)


def group_at(device, place):
    return (((place >> 2) ^ (device & 1)) << 2) | ((place & 3) ^ ((device >> 3) & 3))


def exchange(value, mask_of):
    count = lax.axis_size(AXES)
    return lax.ppermute(value, AXES, [(d, d ^ mask_of(d)) for d in range(count)])


def core_mask(d):
    return 1


def first_mask(d):
    return 2 if d & 1 else 4


def second_mask(d):
    return 4 if d & 1 else 2


def group_order(device):
    place = lax.iota(jnp.int32, GROUPS)
    return (((place >> 2) ^ (device & 1)) << 2) | ((place & 3) ^ ((device >> 3) & 3))


def standard_kernel(samples_total, dosage, keep, counts, projection, standard, projected, turned, gram, kept, rows_in, sketch_in, keep_in, counts_in, table, basis, whole, sems):
    samples = dosage.shape[0]
    steps = samples // ROWS
    device = this_device()
    order = [block_at(device, p) for p in range(BLOCKS)]
    small = [
        pltpu.make_async_copy(source, target, sems.at[i])
        for i, (source, target) in enumerate(((counts, counts_in), (keep, keep_in), (projection, sketch_in)))
    ]
    slabs = [slice(i * ROWS, (i + 1) * ROWS) for i in range(steps)]
    large = [
        pltpu.make_async_copy(dosage.at[slab, :], rows_in.at[slab, :], sems.at[3 + i]) for i, slab in enumerate(slabs)
    ]
    small[0].start()
    small[1].start()
    large[0].start()
    small[2].start()
    for copy in large[1:]:
        copy.start()
    small[0].wait()
    small[1].wait()
    frequency = counts_in[...].astype(jnp.float32) / (2.0 * samples_total)
    table[0] = 2.0 * frequency
    table[1] = 1.0 / jnp.sqrt(2.0 * frequency * (1.0 - frequency))
    for i in range(samples // TILE):
        rows = lax.broadcasted_iota(jnp.int32, (TILE, TILE), 0) + i * TILE
        found = jnp.zeros((TILE, TILE), jnp.float32)
        for j in range(keep.shape[0]):
            found = jnp.where(rows == keep_in[j : j + 1, :], 1.0, found)
        kept[i * TILE : (i + 1) * TILE, :] = jnp.broadcast_to(jnp.max(found, axis=1, keepdims=True), (TILE, TILE))
    for i, slab in enumerate(slabs):
        large[i].wait()
        if i == 0:
            small[2].wait()
            for p in range(BLOCKS):
                start = pl.multiple_of(order[p] * TILE, TILE)
                basis[p * TILE : (p + 1) * TILE, :] = sketch_in[pl.ds(start, TILE), :]
        for p in range(BLOCKS):
            block = order[p]
            center = table[0, pl.ds(block, 1), :]
            scale = table[1, pl.ds(block, 1), :]
            value = rows_in[slab, pl.ds(pl.multiple_of(block * TILE, TILE), TILE)].astype(jnp.float32)
            standard[slab, p * TILE : (p + 1) * TILE] = ((value - center) * scale).astype(jnp.bfloat16)
    value = jnp.dot(standard[...], basis[...], preferred_element_type=jnp.float32)
    finish_rows(value, kept, projected, turned, whole)
    share_gram(whole, gram)


def share_gram(whole, gram):
    device = this_device()
    height = TILE // GROUPS
    for place in range(GROUPS):
        start = pl.multiple_of(group_at(device, place) * height, height)
        gram[place * height : (place + 1) * height, :] = whole[pl.ds(start, height), :]


def finish_rows(value, kept, projected, turned, gram):
    value = jnp.where(kept[...] > 0.0, value, 0.0)
    low = value.astype(jnp.bfloat16)
    low_turned = value.T.astype(jnp.bfloat16)
    projected[...] = low
    turned[...] = low_turned
    gram[...] = jnp.dot(low_turned, low, preferred_element_type=jnp.float32)


ON_CHIP = pl.BlockSpec(memory_space=pltpu.VMEM)
FAR = pl.BlockSpec(memory_space=pltpu.HBM)


def standardize(samples_total, *arrays):
    dosage, keep, counts, projection = [pltpu.with_memory_space_constraint(x, pltpu.HBM) for x in arrays]
    samples, snps = arrays[0].shape
    return pl.pallas_call(
        functools.partial(standard_kernel, samples_total),
        in_specs=[FAR, FAR, FAR, FAR],
        out_specs=[ON_CHIP] * 5,
        out_shape=[
            jax.ShapeDtypeStruct((samples, snps), jnp.bfloat16),
            jax.ShapeDtypeStruct((samples, TILE), jnp.bfloat16),
            jax.ShapeDtypeStruct((TILE, samples), jnp.bfloat16),
            jax.ShapeDtypeStruct((TILE, TILE), jnp.float32),
            jax.ShapeDtypeStruct((samples, TILE), jnp.float32),
        ],
        scratch_shapes=[
            pltpu.VMEM((samples, snps), jnp.bfloat16),
            pltpu.VMEM(arrays[3].shape, jnp.bfloat16),
            pltpu.VMEM(arrays[1].shape, jnp.int32),
            pltpu.VMEM(arrays[2].shape, jnp.int32),
            pltpu.VMEM((2,) + arrays[2].shape, jnp.float32),
            pltpu.VMEM(arrays[3].shape, jnp.bfloat16),
            pltpu.VMEM((TILE, TILE), jnp.float32),
            pltpu.SemaphoreType.DMA((3 + samples // ROWS,)),
        ],
        compiler_params=pltpu.CompilerParams(vmem_limit_bytes=VMEM),
        cost_estimate=pl.CostEstimate(flops=2 * samples * snps * TILE, bytes_accessed=4 * samples * snps, transcendentals=0),
        name="standardize",
    )(dosage, keep, counts, projection)


WIDTH = 512


def totals_kernel(low, high, turned, standard, *refs):
    out = refs[-1]
    base = low * TILE
    for start in range(base, high * TILE, WIDTH):
        value = jnp.dot(turned[...], standard[:, start : start + WIDTH], preferred_element_type=jnp.float32)
        out[start - base : start - base + WIDTH, :] = value.T
    if len(refs) == 2:
        tail = refs[0].shape[0] // 2
        out[(high - low) * TILE :, :] = refs[0][tail:, :]


def totals(turned, standard, low, high, *gram):
    samples = standard.shape[0]
    count = (high - low) * TILE
    tail = TILE // 2 if gram else 0
    return pl.pallas_call(
        functools.partial(totals_kernel, low, high),
        in_specs=[ON_CHIP] * (2 + len(gram)),
        out_specs=ON_CHIP,
        out_shape=jax.ShapeDtypeStruct((count + tail, TILE), jnp.float32),
        compiler_params=pltpu.CompilerParams(vmem_limit_bytes=SMALL),
        cost_estimate=pl.CostEstimate(flops=2 * samples * count * TILE, bytes_accessed=2 * samples * count, transcendentals=0),
        name="totals",
    )(turned, standard, *gram)


def combine_kernel(plan, count, *refs):
    for out, pieces in zip(refs[count:], plan):
        row = 0
        for rows, terms in pieces:
            values = [refs[index][start : start + rows, :] for index, start in terms]
            while len(values) > 1:
                values = [sum(values[i + 1 : i + 2], values[i]) for i in range(0, len(values), 2)]
            out[row : row + rows, :] = values[0]
            row += rows


def combine(arrays, plan):
    shapes = [jax.ShapeDtypeStruct((sum(rows for rows, _ in pieces), TILE), jnp.float32) for pieces in plan]
    size = sum(shape.shape[0] for shape in shapes) * TILE
    return pl.pallas_call(
        functools.partial(combine_kernel, plan, len(arrays)),
        in_specs=[ON_CHIP] * len(arrays),
        out_specs=[ON_CHIP] * len(plan),
        out_shape=shapes,
        compiler_params=pltpu.CompilerParams(vmem_limit_bytes=SMALL),
        cost_estimate=pl.CostEstimate(flops=2 * size, bytes_accessed=12 * size, transcendentals=0),
        name="combine",
    )(*arrays)


def apply_inverse(parts, inverse, basis):
    high, low = split(inverse[...])
    start = 0
    for part in parts:
        size = part.shape[0]
        basis[start : start + size, :] = product(part[...], high, low).astype(jnp.bfloat16)
        start += size


def add_products(standard, basis, base, value):
    row = 0
    for first, count in base:
        size = count * TILE
        term = jnp.dot(
            standard[:, first * TILE : first * TILE + size],
            basis[row : row + size, :],
            preferred_element_type=jnp.float32,
        )
        value = term if value is None else value + term
        row += size
    return value


def begin_kernel(pieces, base, *refs):
    parts = refs[:pieces]
    inverse, standard, out, basis = refs[pieces:]
    apply_inverse(parts, inverse, basis)
    out[...] = add_products(standard, basis, base, None)


def begin_project(parts, base, inverse, standard):
    samples = standard.shape[0]
    rows = sum(part.shape[0] for part in parts)
    return pl.pallas_call(
        functools.partial(begin_kernel, len(parts), base),
        in_specs=[ON_CHIP] * (len(parts) + 2),
        out_specs=ON_CHIP,
        out_shape=jax.ShapeDtypeStruct((samples, TILE), jnp.float32),
        scratch_shapes=[pltpu.VMEM((rows, TILE), jnp.bfloat16)],
        compiler_params=pltpu.CompilerParams(vmem_limit_bytes=SMALL),
        cost_estimate=pl.CostEstimate(flops=2 * samples * rows * TILE, bytes_accessed=2 * samples * rows, transcendentals=0),
        name="begin_project",
    )(*parts, inverse, standard)


def project_kernel(pieces, base, *refs):
    parts = refs[:pieces]
    begun, inverse, standard, kept, projected, turned, gram, basis, whole = refs[pieces:]
    apply_inverse(parts, inverse, basis)
    value = add_products(standard, basis, base, begun[...])
    finish_rows(value, kept, projected, turned, whole)
    share_gram(whole, gram)


def project(parts, base, begun, inverse, standard, kept):
    samples = standard.shape[0]
    rows = sum(part.shape[0] for part in parts)
    return pl.pallas_call(
        functools.partial(project_kernel, len(parts), base),
        in_specs=[ON_CHIP] * (len(parts) + 4),
        out_specs=[ON_CHIP] * 3,
        out_shape=[
            jax.ShapeDtypeStruct((samples, TILE), jnp.bfloat16),
            jax.ShapeDtypeStruct((TILE, samples), jnp.bfloat16),
            jax.ShapeDtypeStruct((TILE, TILE), jnp.float32),
        ],
        scratch_shapes=[pltpu.VMEM((rows, TILE), jnp.bfloat16), pltpu.VMEM((TILE, TILE), jnp.float32)],
        compiler_params=pltpu.CompilerParams(vmem_limit_bytes=SMALL),
        cost_estimate=pl.CostEstimate(flops=2 * samples * rows * TILE, bytes_accessed=2 * samples * rows, transcendentals=0),
        name="project",
    )(*parts, begun, inverse, standard, kept)


PANEL = 16


def eliminate(first, last, left, right, out):
    panel_rows = lax.broadcasted_iota(jnp.int32, (PANEL, TILE), 0)
    for start in range(first, last, PANEL):
        stop = start + PANEL
        upper = left[start:stop, :]
        done = right[start:stop, :]
        columns = [
            jnp.broadcast_to(upper[:, start + j : start + j + 1], (PANEL, TILE)) for j in range(PANEL)
        ]
        for k in range(PANEL):
            pivot = columns[k][k : k + 1, :]
            root = lax.rsqrt(pivot)
            below = jnp.where(panel_rows > k, columns[k] * (root * root), 0.0)
            for j in range(k + 1, PANEL):
                columns[j] = columns[j] - below * columns[j][k : k + 1, :]
            factor = jnp.where(panel_rows == k, root, 1.0)
            upper = upper * factor - below * upper[k : k + 1, :]
            done = done * factor - below * done[k : k + 1, :]
        out[start:stop, :] = done
        if stop < TILE:
            left_parts = thirds(upper)
            right_parts = thirds(jnp.concatenate([upper, done], axis=1))
            pairs = ((0, 0), (0, 1), (1, 0), (0, 2), (1, 1), (2, 0))
            both = lax.dot_general(
                jnp.concatenate([left_parts[i] for i, _ in pairs], axis=0),
                jnp.concatenate([right_parts[j] for _, j in pairs], axis=0),
                (((0,), (0,)), ((), ())),
                preferred_element_type=jnp.float32,
            )
            left[stop:, :] -= both[stop:, :TILE]
            right[stop:, :] -= both[stop:, TILE:]


def begin_kernel_inverse(last, own, other, left, right):
    device = this_device()
    height = TILE // GROUPS
    for half, source in enumerate((own, other)):
        for row in range(GROUPS // 2):
            start = pl.multiple_of(group_at(device, half * (GROUPS // 2) + row) * height, height)
            left[pl.ds(start, height), :] = source[row * height : (row + 1) * height, :]
    lanes = lax.broadcasted_iota(jnp.int32, (TILE, TILE), 1)
    subs = lax.broadcasted_iota(jnp.int32, (TILE, TILE), 0)
    right[...] = jnp.where(lanes == subs, 1.0, 0.0)
    eliminate(0, last, left, right, right)


def end_kernel_inverse(first, left_in, right_in, out, left, right):
    left[first:, :] = left_in[first:, :]
    right[first:, :] = right_in[first:, :]
    out[:first, :] = right_in[:first, :]
    eliminate(first, TILE, left, right, out)


SQUARE = jax.ShapeDtypeStruct((TILE, TILE), jnp.float32)


def begin_inverse(last, own, other):
    return pl.pallas_call(
        functools.partial(begin_kernel_inverse, last),
        in_specs=[ON_CHIP, ON_CHIP],
        out_specs=[ON_CHIP, ON_CHIP],
        out_shape=[SQUARE, SQUARE],
        compiler_params=pltpu.CompilerParams(vmem_limit_bytes=SMALL),
        cost_estimate=pl.CostEstimate(flops=1_000_000_000, bytes_accessed=8_000_000, transcendentals=0),
        name="begin_inverse",
    )(own, other)


def end_inverse(first, left, right):
    return pl.pallas_call(
        functools.partial(end_kernel_inverse, first),
        in_specs=[ON_CHIP, ON_CHIP],
        out_specs=ON_CHIP,
        out_shape=SQUARE,
        scratch_shapes=[pltpu.VMEM((TILE, TILE), jnp.float32), pltpu.VMEM((TILE, TILE), jnp.float32)],
        compiler_params=pltpu.CompilerParams(vmem_limit_bytes=SMALL),
        cost_estimate=pl.CostEstimate(flops=1_000_000_000, bytes_accessed=8_000_000, transcendentals=0),
        name="end_inverse",
    )(left, right)


def invert_factor(own, other):
    return begin_inverse(TILE, own, other)[1]


def pick_kernel(keep, projected, chosen):
    samples = projected.shape[0]
    lanes = lax.broadcasted_iota(jnp.int32, (TILE, samples), 1).astype(jnp.float32)
    for j in range(keep.shape[0]):
        row = jnp.broadcast_to(keep[j : j + 1, :].astype(jnp.float32), (TILE, TILE)).T
        pick = jnp.where(lanes == jnp.tile(row, (1, samples // TILE)), 1.0, 0.0).astype(jnp.bfloat16)
        value = jnp.dot(pick, projected[...], preferred_element_type=jnp.float32)
        chosen[j * TILE : (j + 1) * TILE, :] = value.astype(jnp.bfloat16)


def pick_rows(keep, projected):
    return pl.pallas_call(
        pick_kernel,
        in_specs=[ON_CHIP, ON_CHIP],
        out_specs=ON_CHIP,
        out_shape=jax.ShapeDtypeStruct((keep.shape[0] * TILE, TILE), jnp.bfloat16),
        compiler_params=pltpu.CompilerParams(vmem_limit_bytes=SMALL),
        cost_estimate=pl.CostEstimate(flops=500_000_000, bytes_accessed=4_000_000, transcendentals=0),
        name="pick_rows",
    )(keep, projected)


def scores_kernel(scale, chosen, inverse, scores):
    high, low = split(inverse[...])
    dims = (((1,), (1,)), ((), ()))
    value = lax.dot_general(chosen[...], high, dims, preferred_element_type=jnp.float32)
    value = value + lax.dot_general(chosen[...], low, dims, preferred_element_type=jnp.float32)
    scores[...] = value * scale


def score(scale, chosen, inverse):
    return pl.pallas_call(
        functools.partial(scores_kernel, scale),
        out_shape=jax.ShapeDtypeStruct(chosen.shape, jnp.float32),
        compiler_params=pltpu.CompilerParams(vmem_limit_bytes=SMALL),
        cost_estimate=pl.CostEstimate(flops=500_000_000, bytes_accessed=4_000_000, transcendentals=0),
        name="score",
    )(chosen, inverse)


def loadings_kernel(pieces, positions, *refs):
    wide = lax.axis_index("wide") & 7
    parts = refs[:pieces]
    inverse, loadings = refs[pieces:]
    high, low = split(inverse[...])
    value = product(jnp.concatenate([part[...] for part in parts], axis=0), high, low)
    for i, position in enumerate(positions):
        place = wide ^ (((position & 3) << 1) | (position >> 2))
        start = pl.multiple_of(place * TILE, TILE)
        loadings[pl.ds(start, TILE), :] = value[i * TILE : (i + 1) * TILE, :]


def load(positions, parts, inverse):
    count = sum(part.shape[0] for part in parts)
    return pl.pallas_call(
        functools.partial(loadings_kernel, len(parts), positions),
        in_specs=[ON_CHIP] * (len(parts) + 1),
        out_shape=jax.ShapeDtypeStruct((count, TILE), jnp.float32),
        compiler_params=pltpu.CompilerParams(vmem_limit_bytes=VMEM),
        cost_estimate=pl.CostEstimate(flops=100_000_000, bytes_accessed=1_000_000, transcendentals=0),
        name="load",
    )(*parts, inverse)


def span(rows, *terms):
    return (rows, terms)


def scatter_sum(turned, standard, gram):
    four = 4 * TILE
    eight = 8 * TILE
    slot = TILE // GROUPS
    half = TILE // 2
    three = 3 * TILE
    far = exchange(totals(turned, standard, 24, 32, gram), core_mask)
    upper = totals(turned, standard, 8, 16)
    send, send_rest = combine(
        [upper, far, gram],
        [
            [span(three, (0, four + TILE), (1, four + TILE)), span(half, (2, 0), (1, eight))],
            [span(four + TILE, (0, 0), (1, 0))],
        ],
    )
    first = exchange(send, first_mask)
    rest = exchange(send_rest, first_mask)
    close = exchange(totals(turned, standard, 16, 24), core_mask)
    own = totals(turned, standard, 0, 8)
    (send_next,) = combine(
        [own, close, first, send],
        [[span(three, (0, four + TILE), (1, four + TILE), (2, 0)), span(half, (3, three), (2, three))]],
    )
    second = exchange(send_next, second_mask)
    (send_last,) = combine([own, close, rest], [[span(TILE, (0, four), (1, four), (2, four))]])
    last = exchange(send_last, second_mask)

    def share(q):
        return span(slot, (4, three + q * slot), (3, three + q * slot))

    def packet(q):
        start = q * TILE
        return [span(TILE, (0, start), (1, start), (2, start), (3, start - TILE)), share(q)]

    *packets, own_share = combine(
        [own, close, rest, second, send_next], [packet(q) for q in (3, 2, 1)] + [[share(0)]]
    )
    arrived = [exchange(packet, lambda d, q=q: (3 - q) << 3) for q, packet in enumerate(packets)]
    block = span(TILE, *((i, 0) for i in (0, 1, 2, 3, 5, 6, 7)))
    part = span(slot, (4, 0), (7, TILE), (6, TILE), (5, TILE))
    packet, total = combine([own, close, rest, last, own_share] + arrived, [[block, part], [block]])
    if lax.axis_size(AXES) == BLOCKS:
        return packet, total
    packet = across_rest(packet)
    return packet, packet[:TILE]


def across_rest(value):
    bit = BLOCKS
    while bit < lax.axis_size(AXES):
        value = value + exchange(value, lambda d, bit=bit: bit)
        bit *= 2
    return value


def along_z(value):
    return [exchange(value, lambda d, q=q: q << 3) for q in range(1, 4)]


def gather_near(packet):
    slot = TILE // GROUPS
    return combine(
        [packet] + along_z(packet),
        [[span(TILE, (q, 0)) for q in range(4)], [span(slot, (q, TILE)) for q in range(4)]],
    )


def gather_last(packet, total, mask):
    slot = TILE // GROUPS
    return combine(
        [packet] + along_z(packet) + [exchange(total, mask)],
        [
            [span(TILE, (q, 0)) for q in (1, 2, 3)],
            [span(slot, (q, TILE)) for q in range(4)],
            [span(TILE, (0, 0)), span(TILE, (4, 0))],
        ],
    )


def on_device(dosage, keep_rows, allele_counts, projection):
    groups = lax.axis_size(AXES)
    samples_total = dosage.shape[0] * groups
    kept_total = keep_rows.shape[0] * groups
    keep = keep_rows.reshape(-1, TILE)
    counts = allele_counts.reshape(-1, TILE)
    standard, _, turned, gram, kept = standardize(samples_total, dosage, keep, counts, projection)
    packet, _ = scatter_sum(turned, standard, gram)
    near, share = gather_near(packet)
    across = exchange(near, second_mask)
    other = exchange(share, core_mask)
    later, other = lax.optimization_barrier((near, other))
    along = exchange(later, first_mask)
    middle = begin_inverse(HALF, share, other)
    across, middle = lax.optimization_barrier((across, middle))
    corner = exchange(across, first_mask)
    inverse = end_inverse(HALF, *middle)
    early = [near, across, along] + [exchange(part, core_mask) for part in (near, across)]
    begun = begin_project(early, [(0, 4), (4, 4), (8, 4), (16, 4), (20, 4)], inverse, standard)
    corner, begun = lax.optimization_barrier((corner, begun))
    late = [exchange(along, core_mask), corner, exchange(corner, core_mask)]
    ranges = [(24, 4), (12, 4), (28, 4)]
    projected, turned, gram = project(late, ranges, begun, inverse, standard, kept)
    packet, total = scatter_sum(turned, standard, gram)
    chosen = pick_rows(keep, projected)
    packet, total, chosen = lax.optimization_barrier((packet, total, chosen))
    near, share, corners = gather_last(packet, total, lambda d: 4)
    beside = exchange(near, lambda d: 4)
    inverse = invert_factor(share, exchange(share, core_mask))
    scores = score(math.sqrt(kept_total), chosen, inverse)
    loadings = load((0, 4, 1, 2, 3, 5, 6, 7), [corners, near, beside], inverse)
    return (scores, loadings)


def solution(mesh):
    in_specs = (P(AXES, None), P(AXES), P(), P())
    out_specs = (P(AXES, None), P("narrow", None))
    return jax.shard_map(
        on_device, mesh=mesh, in_specs=in_specs, out_specs=out_specs, check_vma=False
    )
```

```python
import functools
import math

import jax
import jax.numpy as jnp
from jax import lax
from jax.experimental import pallas as pl
from jax.experimental.pallas import tpu as pltpu
from jax.sharding import PartitionSpec as P

AXES = ("wide", "narrow")
TILE = 128
BLOCKS = 32
ROWS = 256
STRIP = 64
SPLIT = 96
VMEM = 28 * 1024 * 1024
SMALL = 16 * 1024 * 1024
GROUPS = 8
HALF = TILE // 2


def split(value):
    high = value.astype(jnp.bfloat16)
    low = (value - high.astype(jnp.float32)).astype(jnp.bfloat16)
    return high, low


def thirds(value):
    high = value.astype(jnp.bfloat16)
    return (high,) + split(value - high.astype(jnp.float32))


def product(left, right_high, right_low):
    high, low = split(left)
    dims = (((1,), (1,)), ((), ()))
    dot = functools.partial(lax.dot_general, dimension_numbers=dims, preferred_element_type=jnp.float32)
    return dot(high, right_high) + (dot(high, right_low) + dot(low, right_high))


def relative(position, core):
    first = (position >> 3) & 1
    second = (position >> 2) & 1
    core_bit = (position >> 4) & 1
    target = core ^ core_bit
    bit_x = first * (1 - target) + second * target
    bit_y = second * (1 - target) + first * target
    return core_bit | (bit_y << 1) | (bit_x << 2) | ((position & 3) << 3)


def this_device():
    return lax.axis_index("wide") * lax.axis_size("narrow") + lax.axis_index("narrow")


def block_at(device, position):
    owner = device ^ relative(position, device & 1)
    return (owner & 3) * 8 + ((owner >> 2) & 7)


def group_at(device, place):
    return (((place >> 2) ^ (device & 1)) << 2) | ((place & 3) ^ ((device >> 3) & 3))


def exchange(value, mask_of):
    count = lax.axis_size(AXES)
    return lax.ppermute(value, AXES, [(d, d ^ mask_of(d)) for d in range(count)])


def core_mask(d):
    return 1


def first_mask(d):
    return 2 if d & 1 else 4


def second_mask(d):
    return 4 if d & 1 else 2


def group_order(device):
    place = lax.iota(jnp.int32, GROUPS)
    return (((place >> 2) ^ (device & 1)) << 2) | ((place & 3) ^ ((device >> 3) & 3))


def standard_kernel(samples_total, dosage, keep, counts, projection, standard, projected, turned, gram, kept, far, rows_in, sketch_in, keep_in, counts_in, table, basis, whole, sems):
    samples = dosage.shape[0]
    steps = samples // ROWS
    device = this_device()
    order = [block_at(device, p) for p in range(BLOCKS)]
    small = [
        pltpu.make_async_copy(source, target, sems.at[i])
        for i, (source, target) in enumerate(((counts, counts_in), (keep, keep_in), (projection, sketch_in)))
    ]
    slabs = [slice(i * ROWS, (i + 1) * ROWS) for i in range(steps)]
    large = [
        pltpu.make_async_copy(dosage.at[slab, :], rows_in.at[slab, :], sems.at[3 + i]) for i, slab in enumerate(slabs)
    ]
    small[0].start()
    small[1].start()
    large[0].start()
    small[2].start()
    for copy in large[1:]:
        copy.start()
    small[0].wait()
    small[1].wait()
    frequency = counts_in[...].astype(jnp.float32) / (2.0 * samples_total)
    table[0] = 2.0 * frequency
    table[1] = 1.0 / jnp.sqrt(2.0 * frequency * (1.0 - frequency))
    for p in range(BLOCKS):
        table[2, p : p + 1, :] = table[0, pl.ds(order[p], 1), :]
        table[3, p : p + 1, :] = table[1, pl.ds(order[p], 1), :]
    for i in range(samples // TILE):
        rows = lax.broadcasted_iota(jnp.int32, (TILE, TILE), 0) + i * TILE
        found = jnp.zeros((TILE, TILE), jnp.float32)
        for j in range(keep.shape[0]):
            found = jnp.where(rows == keep_in[j : j + 1, :], 1.0, found)
        kept[i * TILE : (i + 1) * TILE, :] = jnp.broadcast_to(jnp.max(found, axis=1, keepdims=True), (TILE, TILE))
    for i, slab in enumerate(slabs):
        large[i].wait()
        if i == 0:
            small[2].wait()
            for p in range(BLOCKS):
                start = pl.multiple_of(order[p] * TILE, TILE)
                basis[p * TILE : (p + 1) * TILE, :] = sketch_in[pl.ds(start, TILE), :]
        for row in range(slab.start, slab.stop, STRIP):
            strip = slice(row, row + STRIP)
            for p in range(BLOCKS):
                value = rows_in[strip, pl.ds(pl.multiple_of(order[p] * TILE, TILE), TILE)].astype(jnp.float32)
                value = (value - table[2, p : p + 1, :]) * table[3, p : p + 1, :]
                standard[strip, p * TILE : (p + 1) * TILE] = value.astype(jnp.bfloat16)
    value = jnp.dot(standard[...], basis[...], preferred_element_type=jnp.float32)
    finish_rows(value, kept, projected, turned, whole)
    share_gram(whole, gram)
    totals_kernel(24, 32, turned, standard, gram, far)


def share_gram(whole, gram):
    device = this_device()
    height = TILE // GROUPS
    for place in range(GROUPS):
        start = pl.multiple_of(group_at(device, place) * height, height)
        gram[place * height : (place + 1) * height, :] = whole[pl.ds(start, height), :]


def finish_rows(value, kept, projected, turned, gram):
    value = jnp.where(kept[...] > 0.0, value, 0.0)
    low = value.astype(jnp.bfloat16)
    low_turned = value.T.astype(jnp.bfloat16)
    projected[...] = low
    turned[...] = low_turned
    gram[...] = jnp.dot(low_turned, low, preferred_element_type=jnp.float32)


ON_CHIP = pl.BlockSpec(memory_space=pltpu.VMEM)
FAR = pl.BlockSpec(memory_space=pltpu.HBM)


def standardize(samples_total, *arrays):
    dosage, keep, counts, projection = [pltpu.with_memory_space_constraint(x, pltpu.HBM) for x in arrays]
    samples, snps = arrays[0].shape
    return pl.pallas_call(
        functools.partial(standard_kernel, samples_total),
        in_specs=[FAR, FAR, FAR, FAR],
        out_specs=[ON_CHIP] * 6,
        out_shape=[
            jax.ShapeDtypeStruct((samples, snps), jnp.bfloat16),
            jax.ShapeDtypeStruct((samples, TILE), jnp.bfloat16),
            jax.ShapeDtypeStruct((TILE, samples), jnp.bfloat16),
            jax.ShapeDtypeStruct((TILE, TILE), jnp.float32),
            jax.ShapeDtypeStruct((samples, TILE), jnp.float32),
            jax.ShapeDtypeStruct((8 * TILE + HALF, TILE), jnp.float32),
        ],
        scratch_shapes=[
            pltpu.VMEM((samples, snps), jnp.bfloat16),
            pltpu.VMEM(arrays[3].shape, jnp.bfloat16),
            pltpu.VMEM(arrays[1].shape, jnp.int32),
            pltpu.VMEM(arrays[2].shape, jnp.int32),
            pltpu.VMEM((4,) + arrays[2].shape, jnp.float32),
            pltpu.VMEM(arrays[3].shape, jnp.bfloat16),
            pltpu.VMEM((TILE, TILE), jnp.float32),
            pltpu.SemaphoreType.DMA((3 + samples // ROWS,)),
        ],
        compiler_params=pltpu.CompilerParams(vmem_limit_bytes=VMEM),
        cost_estimate=pl.CostEstimate(flops=2 * samples * snps * TILE, bytes_accessed=4 * samples * snps, transcendentals=0),
        name="standardize",
    )(dosage, keep, counts, projection)


WIDTH = 512


def totals_kernel(low, high, turned, standard, *refs):
    out = refs[-1]
    base = low * TILE
    for start in range(base, high * TILE, WIDTH):
        value = jnp.dot(turned[...], standard[:, start : start + WIDTH], preferred_element_type=jnp.float32)
        out[start - base : start - base + WIDTH, :] = value.T
    if len(refs) == 2:
        tail = refs[0].shape[0] // 2
        out[(high - low) * TILE :, :] = refs[0][tail:, :]


def totals(turned, standard, low, high, *gram):
    samples = standard.shape[0]
    count = (high - low) * TILE
    tail = TILE // 2 if gram else 0
    return pl.pallas_call(
        functools.partial(totals_kernel, low, high),
        in_specs=[ON_CHIP] * (2 + len(gram)),
        out_specs=ON_CHIP,
        out_shape=jax.ShapeDtypeStruct((count + tail, TILE), jnp.float32),
        compiler_params=pltpu.CompilerParams(vmem_limit_bytes=SMALL),
        cost_estimate=pl.CostEstimate(flops=2 * samples * count * TILE, bytes_accessed=2 * samples * count, transcendentals=0),
        name="totals",
    )(turned, standard, *gram)


def combine_kernel(plan, count, *refs):
    for out, pieces in zip(refs[count:], plan):
        row = 0
        for rows, terms in pieces:
            values = [refs[index][start : start + rows, :] for index, start in terms]
            while len(values) > 1:
                values = [sum(values[i + 1 : i + 2], values[i]) for i in range(0, len(values), 2)]
            out[row : row + rows, :] = values[0]
            row += rows


def combine(arrays, plan):
    shapes = [jax.ShapeDtypeStruct((sum(rows for rows, _ in pieces), TILE), jnp.float32) for pieces in plan]
    size = sum(shape.shape[0] for shape in shapes) * TILE
    return pl.pallas_call(
        functools.partial(combine_kernel, plan, len(arrays)),
        in_specs=[ON_CHIP] * len(arrays),
        out_specs=[ON_CHIP] * len(plan),
        out_shape=shapes,
        compiler_params=pltpu.CompilerParams(vmem_limit_bytes=SMALL),
        cost_estimate=pl.CostEstimate(flops=2 * size, bytes_accessed=12 * size, transcendentals=0),
        name="combine",
    )(*arrays)


def apply_inverse(parts, inverse, basis):
    high, low = split(inverse[...])
    start = 0
    for part in parts:
        size = part.shape[0]
        basis[start : start + size, :] = product(part[...], high, low).astype(jnp.bfloat16)
        start += size


def add_products(standard, basis, base, value):
    row = 0
    for first, count in base:
        size = count * TILE
        term = jnp.dot(
            standard[:, first * TILE : first * TILE + size],
            basis[row : row + size, :],
            preferred_element_type=jnp.float32,
        )
        value = term if value is None else value + term
        row += size
    return value


def begin_kernel(pieces, base, *refs):
    parts = refs[:pieces]
    inverse, standard, out, basis = refs[pieces:]
    apply_inverse(parts, inverse, basis)
    out[...] = add_products(standard, basis, base, None)


def begin_project(parts, base, inverse, standard):
    samples = standard.shape[0]
    rows = sum(part.shape[0] for part in parts)
    return pl.pallas_call(
        functools.partial(begin_kernel, len(parts), base),
        in_specs=[ON_CHIP] * (len(parts) + 2),
        out_specs=ON_CHIP,
        out_shape=jax.ShapeDtypeStruct((samples, TILE), jnp.float32),
        scratch_shapes=[pltpu.VMEM((rows, TILE), jnp.bfloat16)],
        compiler_params=pltpu.CompilerParams(vmem_limit_bytes=SMALL),
        cost_estimate=pl.CostEstimate(flops=2 * samples * rows * TILE, bytes_accessed=2 * samples * rows, transcendentals=0),
        name="begin_project",
    )(*parts, inverse, standard)


def project_kernel(pieces, base, *refs):
    parts = refs[:pieces]
    begun, inverse, standard, kept, projected, turned, gram, basis, whole = refs[pieces:]
    apply_inverse(parts, inverse, basis)
    value = add_products(standard, basis, base, begun[...])
    finish_rows(value, kept, projected, turned, whole)
    share_gram(whole, gram)


def project(parts, base, begun, inverse, standard, kept):
    samples = standard.shape[0]
    rows = sum(part.shape[0] for part in parts)
    return pl.pallas_call(
        functools.partial(project_kernel, len(parts), base),
        in_specs=[ON_CHIP] * (len(parts) + 4),
        out_specs=[ON_CHIP] * 3,
        out_shape=[
            jax.ShapeDtypeStruct((samples, TILE), jnp.bfloat16),
            jax.ShapeDtypeStruct((TILE, samples), jnp.bfloat16),
            jax.ShapeDtypeStruct((TILE, TILE), jnp.float32),
        ],
        scratch_shapes=[pltpu.VMEM((rows, TILE), jnp.bfloat16), pltpu.VMEM((TILE, TILE), jnp.float32)],
        compiler_params=pltpu.CompilerParams(vmem_limit_bytes=SMALL),
        cost_estimate=pl.CostEstimate(flops=2 * samples * rows * TILE, bytes_accessed=2 * samples * rows, transcendentals=0),
        name="project",
    )(*parts, begun, inverse, standard, kept)


PANEL = 16


def eliminate(first, last, left, right, out):
    panel_rows = lax.broadcasted_iota(jnp.int32, (PANEL, TILE), 0)
    for start in range(first, last, PANEL):
        stop = start + PANEL
        upper = left[start:stop, :]
        done = right[start:stop, :]
        columns = [
            jnp.broadcast_to(upper[:, start + j : start + j + 1], (PANEL, TILE)) for j in range(PANEL)
        ]
        for k in range(PANEL):
            pivot = columns[k][k : k + 1, :]
            root = lax.rsqrt(pivot)
            below = jnp.where(panel_rows > k, columns[k] * (root * root), 0.0)
            for j in range(k + 1, PANEL):
                columns[j] = columns[j] - below * columns[j][k : k + 1, :]
            factor = jnp.where(panel_rows == k, root, 1.0)
            upper = upper * factor - below * upper[k : k + 1, :]
            done = done * factor - below * done[k : k + 1, :]
        out[start:stop, :] = done
        if stop < TILE:
            left_parts = thirds(upper)
            right_parts = thirds(jnp.concatenate([upper, done], axis=1))
            pairs = ((0, 0), (0, 1), (1, 0), (0, 2), (1, 1), (2, 0))
            both = lax.dot_general(
                jnp.concatenate([left_parts[i] for i, _ in pairs], axis=0),
                jnp.concatenate([right_parts[j] for _, j in pairs], axis=0),
                (((0,), (0,)), ((), ())),
                preferred_element_type=jnp.float32,
            )
            left[stop:, :] -= both[stop:, :TILE]
            right[stop:, :] -= both[stop:, TILE:]


def begin_kernel_inverse(last, own, other, left, right):
    device = this_device()
    height = TILE // GROUPS
    for half, source in enumerate((own, other)):
        for row in range(GROUPS // 2):
            start = pl.multiple_of(group_at(device, half * (GROUPS // 2) + row) * height, height)
            left[pl.ds(start, height), :] = source[row * height : (row + 1) * height, :]
    lanes = lax.broadcasted_iota(jnp.int32, (TILE, TILE), 1)
    subs = lax.broadcasted_iota(jnp.int32, (TILE, TILE), 0)
    right[...] = jnp.where(lanes == subs, 1.0, 0.0)
    eliminate(0, last, left, right, right)


def end_kernel_inverse(first, left_in, right_in, out, left, right):
    left[first:, :] = left_in[first:, :]
    right[first:, :] = right_in[first:, :]
    out[:first, :] = right_in[:first, :]
    eliminate(first, TILE, left, right, out)


SQUARE = jax.ShapeDtypeStruct((TILE, TILE), jnp.float32)


def begin_inverse(last, own, other):
    return pl.pallas_call(
        functools.partial(begin_kernel_inverse, last),
        in_specs=[ON_CHIP, ON_CHIP],
        out_specs=[ON_CHIP, ON_CHIP],
        out_shape=[SQUARE, SQUARE],
        compiler_params=pltpu.CompilerParams(vmem_limit_bytes=SMALL),
        cost_estimate=pl.CostEstimate(flops=1_000_000_000, bytes_accessed=8_000_000, transcendentals=0),
        name="begin_inverse",
    )(own, other)


def end_inverse(first, left, right):
    return pl.pallas_call(
        functools.partial(end_kernel_inverse, first),
        in_specs=[ON_CHIP, ON_CHIP],
        out_specs=ON_CHIP,
        out_shape=SQUARE,
        scratch_shapes=[pltpu.VMEM((TILE, TILE), jnp.float32), pltpu.VMEM((TILE, TILE), jnp.float32)],
        compiler_params=pltpu.CompilerParams(vmem_limit_bytes=SMALL),
        cost_estimate=pl.CostEstimate(flops=1_000_000_000, bytes_accessed=8_000_000, transcendentals=0),
        name="end_inverse",
    )(left, right)


def invert_factor(own, other):
    return begin_inverse(TILE, own, other)[1]


def pick_kernel(keep, projected, chosen):
    samples = projected.shape[0]
    lanes = lax.broadcasted_iota(jnp.int32, (TILE, samples), 1).astype(jnp.float32)
    for j in range(keep.shape[0]):
        row = jnp.broadcast_to(keep[j : j + 1, :].astype(jnp.float32), (TILE, TILE)).T
        pick = jnp.where(lanes == jnp.tile(row, (1, samples // TILE)), 1.0, 0.0).astype(jnp.bfloat16)
        value = jnp.dot(pick, projected[...], preferred_element_type=jnp.float32)
        chosen[j * TILE : (j + 1) * TILE, :] = value.astype(jnp.bfloat16)


def pick_rows(keep, projected):
    return pl.pallas_call(
        pick_kernel,
        in_specs=[ON_CHIP, ON_CHIP],
        out_specs=ON_CHIP,
        out_shape=jax.ShapeDtypeStruct((keep.shape[0] * TILE, TILE), jnp.bfloat16),
        compiler_params=pltpu.CompilerParams(vmem_limit_bytes=SMALL),
        cost_estimate=pl.CostEstimate(flops=500_000_000, bytes_accessed=4_000_000, transcendentals=0),
        name="pick_rows",
    )(keep, projected)


def scores_kernel(scale, chosen, inverse, scores):
    high, low = split(inverse[...])
    dims = (((1,), (1,)), ((), ()))
    value = lax.dot_general(chosen[...], high, dims, preferred_element_type=jnp.float32)
    value = value + lax.dot_general(chosen[...], low, dims, preferred_element_type=jnp.float32)
    scores[...] = value * scale


def score(scale, chosen, inverse):
    return pl.pallas_call(
        functools.partial(scores_kernel, scale),
        out_shape=jax.ShapeDtypeStruct(chosen.shape, jnp.float32),
        compiler_params=pltpu.CompilerParams(vmem_limit_bytes=SMALL),
        cost_estimate=pl.CostEstimate(flops=500_000_000, bytes_accessed=4_000_000, transcendentals=0),
        name="score",
    )(chosen, inverse)


def loadings_kernel(pieces, positions, *refs):
    wide = lax.axis_index("wide") & 7
    parts = refs[:pieces]
    inverse, loadings = refs[pieces:]
    high, low = split(inverse[...])
    value = product(jnp.concatenate([part[...] for part in parts], axis=0), high, low)
    for i, position in enumerate(positions):
        place = wide ^ (((position & 3) << 1) | (position >> 2))
        start = pl.multiple_of(place * TILE, TILE)
        loadings[pl.ds(start, TILE), :] = value[i * TILE : (i + 1) * TILE, :]


def load(positions, parts, inverse):
    count = sum(part.shape[0] for part in parts)
    return pl.pallas_call(
        functools.partial(loadings_kernel, len(parts), positions),
        in_specs=[ON_CHIP] * (len(parts) + 1),
        out_shape=jax.ShapeDtypeStruct((count, TILE), jnp.float32),
        compiler_params=pltpu.CompilerParams(vmem_limit_bytes=VMEM),
        cost_estimate=pl.CostEstimate(flops=100_000_000, bytes_accessed=1_000_000, transcendentals=0),
        name="load",
    )(*parts, inverse)


def span(rows, *terms):
    return (rows, terms)


def scatter_sum(turned, standard, gram, far):
    four = 4 * TILE
    eight = 8 * TILE
    slot = TILE // GROUPS
    half = TILE // 2
    three = 3 * TILE
    far = exchange(far, core_mask)
    upper = totals(turned, standard, 8, 16)
    send, send_rest = combine(
        [upper, far, gram],
        [
            [span(three, (0, four + TILE), (1, four + TILE)), span(half, (2, 0), (1, eight))],
            [span(four + TILE, (0, 0), (1, 0))],
        ],
    )
    first = exchange(send, first_mask)
    rest = exchange(send_rest, first_mask)
    close = exchange(totals(turned, standard, 16, 24), core_mask)
    own = totals(turned, standard, 0, 8)
    (send_next,) = combine(
        [own, close, first, send],
        [[span(three, (0, four + TILE), (1, four + TILE), (2, 0)), span(half, (3, three), (2, three))]],
    )
    second = exchange(send_next, second_mask)
    (send_last,) = combine([own, close, rest], [[span(TILE, (0, four), (1, four), (2, four))]])
    last = exchange(send_last, second_mask)

    def share(q):
        return span(slot, (4, three + q * slot), (3, three + q * slot))

    def packet(q):
        start = q * TILE
        return [span(TILE, (0, start), (1, start), (2, start), (3, start - TILE)), share(q)]

    *packets, own_share = combine(
        [own, close, rest, second, send_next], [packet(q) for q in (3, 2, 1)] + [[share(0)]]
    )
    arrived = [exchange(packet, lambda d, q=q: (3 - q) << 3) for q, packet in enumerate(packets)]
    block = span(TILE, *((i, 0) for i in (0, 1, 2, 3, 5, 6, 7)))
    part = span(slot, (4, 0), (7, TILE), (6, TILE), (5, TILE))
    packet, total = combine([own, close, rest, last, own_share] + arrived, [[block, part], [block]])
    if lax.axis_size(AXES) == BLOCKS:
        return packet, total
    packet = across_rest(packet)
    return packet, packet[:TILE]


def across_rest(value):
    bit = BLOCKS
    while bit < lax.axis_size(AXES):
        value = value + exchange(value, lambda d, bit=bit: bit)
        bit *= 2
    return value


def along_z(value):
    return [exchange(value, lambda d, q=q: q << 3) for q in range(1, 4)]


def gather_near(packet):
    slot = TILE // GROUPS
    return combine(
        [packet] + along_z(packet),
        [[span(TILE, (q, 0)) for q in range(4)], [span(slot, (q, TILE)) for q in range(4)]],
    )


def gather_last(packet, total, mask):
    slot = TILE // GROUPS
    return combine(
        [packet] + along_z(packet) + [exchange(total, mask)],
        [
            [span(TILE, (q, 0)) for q in (1, 2, 3)],
            [span(slot, (q, TILE)) for q in range(4)],
            [span(TILE, (0, 0)), span(TILE, (4, 0))],
        ],
    )


def on_device(dosage, keep_rows, allele_counts, projection):
    groups = lax.axis_size(AXES)
    samples_total = dosage.shape[0] * groups
    kept_total = keep_rows.shape[0] * groups
    keep = keep_rows.reshape(-1, TILE)
    counts = allele_counts.reshape(-1, TILE)
    standard, _, turned, gram, kept, far = standardize(samples_total, dosage, keep, counts, projection)
    packet, _ = scatter_sum(turned, standard, gram, far)
    near, share = gather_near(packet)
    across = exchange(near, second_mask)
    other = exchange(share, core_mask)
    later, other = lax.optimization_barrier((near, other))
    along = exchange(later, first_mask)
    middle = begin_inverse(SPLIT, share, other)
    across, middle = lax.optimization_barrier((across, middle))
    corner = exchange(across, first_mask)
    inverse = end_inverse(SPLIT, *middle)
    early = [near, across, along] + [exchange(part, core_mask) for part in (near, across)]
    begun = begin_project(early, [(0, 4), (4, 4), (8, 4), (16, 4), (20, 4)], inverse, standard)
    corner, begun = lax.optimization_barrier((corner, begun))
    late = [exchange(along, core_mask), corner, exchange(corner, core_mask)]
    ranges = [(24, 4), (12, 4), (28, 4)]
    projected, turned, gram = project(late, ranges, begun, inverse, standard, kept)
    packet, total = scatter_sum(turned, standard, gram, totals(turned, standard, 24, 32, gram))
    chosen = pick_rows(keep, projected)
    packet, total, chosen = lax.optimization_barrier((packet, total, chosen))
    near, share, corners = gather_last(packet, total, lambda d: 4)
    beside = exchange(near, lambda d: 4)
    inverse = invert_factor(share, exchange(share, core_mask))
    scores = score(math.sqrt(kept_total), chosen, inverse)
    loadings = load((0, 4, 1, 2, 3, 5, 6, 7), [corners, near, beside], inverse)
    return (scores, loadings)


def solution(mesh):
    in_specs = (P(AXES, None), P(AXES), P(), P())
    out_specs = (P(AXES, None), P("narrow", None))
    return jax.shard_map(
        on_device, mesh=mesh, in_specs=in_specs, out_specs=out_specs, check_vma=False
    )
```

```python
import functools
import math

import jax
import jax.numpy as jnp
from jax import lax
from jax.experimental import pallas as pl
from jax.experimental.pallas import tpu as pltpu
from jax.sharding import PartitionSpec as P

AXES = ("wide", "narrow")
TILE = 128
BLOCKS = 32
ROWS = 256
STRIP = 64
SPLIT = 96
VMEM = 28 * 1024 * 1024
SMALL = 16 * 1024 * 1024
GROUPS = 8
HALF = TILE // 2


def split(value):
    high = value.astype(jnp.bfloat16)
    low = (value - high.astype(jnp.float32)).astype(jnp.bfloat16)
    return high, low


def thirds(value):
    high = value.astype(jnp.bfloat16)
    return (high,) + split(value - high.astype(jnp.float32))


def product(left, right_high, right_low):
    high, low = split(left)
    dims = (((1,), (1,)), ((), ()))
    dot = functools.partial(lax.dot_general, dimension_numbers=dims, preferred_element_type=jnp.float32)
    return dot(high, right_high) + (dot(high, right_low) + dot(low, right_high))


def relative(position, core):
    first = (position >> 3) & 1
    second = (position >> 2) & 1
    core_bit = (position >> 4) & 1
    target = core ^ core_bit
    bit_x = first * (1 - target) + second * target
    bit_y = second * (1 - target) + first * target
    return core_bit | (bit_y << 1) | (bit_x << 2) | ((position & 3) << 3)


def this_device():
    return lax.axis_index("wide") * lax.axis_size("narrow") + lax.axis_index("narrow")


def block_at(device, position):
    owner = device ^ relative(position, device & 1)
    return (owner & 3) * 8 + ((owner >> 2) & 7)


def group_at(device, place):
    return (((place >> 2) ^ (device & 1)) << 2) | ((place & 3) ^ ((device >> 3) & 3))


def exchange(value, mask_of):
    count = lax.axis_size(AXES)
    return lax.ppermute(value, AXES, [(d, d ^ mask_of(d)) for d in range(count)])


def core_mask(d):
    return 1


def first_mask(d):
    return 2 if d & 1 else 4


def second_mask(d):
    return 4 if d & 1 else 2


def group_order(device):
    place = lax.iota(jnp.int32, GROUPS)
    return (((place >> 2) ^ (device & 1)) << 2) | ((place & 3) ^ ((device >> 3) & 3))


def standard_kernel(samples_total, dosage, keep, counts, projection, standard, projected, turned, gram, kept, far, rows_in, sketch_in, keep_in, counts_in, table, basis, whole, sems):
    samples = dosage.shape[0]
    steps = samples // ROWS
    device = this_device()
    order = [block_at(device, p) for p in range(BLOCKS)]
    small = [
        pltpu.make_async_copy(source, target, sems.at[i])
        for i, (source, target) in enumerate(((counts, counts_in), (keep, keep_in), (projection, sketch_in)))
    ]
    slabs = [slice(i * ROWS, (i + 1) * ROWS) for i in range(steps)]
    large = [
        pltpu.make_async_copy(dosage.at[slab, :], rows_in.at[slab, :], sems.at[3 + i]) for i, slab in enumerate(slabs)
    ]
    small[0].start()
    small[1].start()
    large[0].start()
    small[2].start()
    for copy in large[1:]:
        copy.start()
    small[0].wait()
    small[1].wait()
    frequency = counts_in[...].astype(jnp.float32) / (2.0 * samples_total)
    table[0] = 2.0 * frequency
    table[1] = 1.0 / jnp.sqrt(2.0 * frequency * (1.0 - frequency))
    for p in range(BLOCKS):
        table[2, p : p + 1, :] = table[0, pl.ds(order[p], 1), :]
        table[3, p : p + 1, :] = table[1, pl.ds(order[p], 1), :]
    for i in range(samples // TILE):
        rows = lax.broadcasted_iota(jnp.int32, (TILE, TILE), 0) + i * TILE
        found = jnp.zeros((TILE, TILE), jnp.float32)
        for j in range(keep.shape[0]):
            found = jnp.where(rows == keep_in[j : j + 1, :], 1.0, found)
        kept[i * TILE : (i + 1) * TILE, :] = jnp.broadcast_to(jnp.max(found, axis=1, keepdims=True), (TILE, TILE))
    for i, slab in enumerate(slabs):
        large[i].wait()
        if i == 0:
            small[2].wait()
            for p in range(BLOCKS):
                start = pl.multiple_of(order[p] * TILE, TILE)
                basis[p * TILE : (p + 1) * TILE, :] = sketch_in[pl.ds(start, TILE), :]
        for row in range(slab.start, slab.stop, STRIP):
            strip = slice(row, row + STRIP)
            for p in range(BLOCKS):
                value = rows_in[strip, pl.ds(pl.multiple_of(order[p] * TILE, TILE), TILE)].astype(jnp.float32)
                value = (value - table[2, p : p + 1, :]) * table[3, p : p + 1, :]
                standard[strip, p * TILE : (p + 1) * TILE] = value.astype(jnp.bfloat16)
    value = jnp.dot(standard[...], basis[...], preferred_element_type=jnp.float32)
    finish_rows(value, kept, projected, turned, whole)
    share_gram(whole, gram)
    totals_kernel(24, 32, turned, standard, gram, far)


def share_gram(whole, gram):
    device = this_device()
    height = TILE // GROUPS
    for place in range(GROUPS):
        start = pl.multiple_of(group_at(device, place) * height, height)
        gram[place * height : (place + 1) * height, :] = whole[pl.ds(start, height), :]


def finish_rows(value, kept, projected, turned, gram):
    value = jnp.where(kept[...] > 0.0, value, 0.0)
    low = value.astype(jnp.bfloat16)
    low_turned = value.T.astype(jnp.bfloat16)
    projected[...] = low
    turned[...] = low_turned
    gram[...] = jnp.dot(low_turned, low, preferred_element_type=jnp.float32)


ON_CHIP = pl.BlockSpec(memory_space=pltpu.VMEM)
FAR = pl.BlockSpec(memory_space=pltpu.HBM)


def standardize(samples_total, *arrays):
    dosage, keep, counts, projection = [pltpu.with_memory_space_constraint(x, pltpu.HBM) for x in arrays]
    samples, snps = arrays[0].shape
    return pl.pallas_call(
        functools.partial(standard_kernel, samples_total),
        in_specs=[FAR, FAR, FAR, FAR],
        out_specs=[ON_CHIP] * 6,
        out_shape=[
            jax.ShapeDtypeStruct((samples, snps), jnp.bfloat16),
            jax.ShapeDtypeStruct((samples, TILE), jnp.bfloat16),
            jax.ShapeDtypeStruct((TILE, samples), jnp.bfloat16),
            jax.ShapeDtypeStruct((TILE, TILE), jnp.float32),
            jax.ShapeDtypeStruct((samples, TILE), jnp.float32),
            jax.ShapeDtypeStruct((8 * TILE + HALF, TILE), jnp.float32),
        ],
        scratch_shapes=[
            pltpu.VMEM((samples, snps), jnp.bfloat16),
            pltpu.VMEM(arrays[3].shape, jnp.bfloat16),
            pltpu.VMEM(arrays[1].shape, jnp.int32),
            pltpu.VMEM(arrays[2].shape, jnp.int32),
            pltpu.VMEM((4,) + arrays[2].shape, jnp.float32),
            pltpu.VMEM(arrays[3].shape, jnp.bfloat16),
            pltpu.VMEM((TILE, TILE), jnp.float32),
            pltpu.SemaphoreType.DMA((3 + samples // ROWS,)),
        ],
        compiler_params=pltpu.CompilerParams(vmem_limit_bytes=VMEM),
        cost_estimate=pl.CostEstimate(flops=2 * samples * snps * TILE, bytes_accessed=4 * samples * snps, transcendentals=0),
        name="standardize",
    )(dosage, keep, counts, projection)


WIDTH = 512


def totals_kernel(low, high, turned, standard, *refs):
    out = refs[-1]
    base = low * TILE
    for start in range(base, high * TILE, WIDTH):
        value = jnp.dot(turned[...], standard[:, start : start + WIDTH], preferred_element_type=jnp.float32)
        out[start - base : start - base + WIDTH, :] = value.T
    if len(refs) == 2:
        tail = refs[0].shape[0] // 2
        out[(high - low) * TILE :, :] = refs[0][tail:, :]


def totals(turned, standard, low, high, *gram):
    samples = standard.shape[0]
    count = (high - low) * TILE
    tail = TILE // 2 if gram else 0
    return pl.pallas_call(
        functools.partial(totals_kernel, low, high),
        in_specs=[ON_CHIP] * (2 + len(gram)),
        out_specs=ON_CHIP,
        out_shape=jax.ShapeDtypeStruct((count + tail, TILE), jnp.float32),
        compiler_params=pltpu.CompilerParams(vmem_limit_bytes=SMALL),
        cost_estimate=pl.CostEstimate(flops=2 * samples * count * TILE, bytes_accessed=2 * samples * count, transcendentals=0),
        name="totals",
    )(turned, standard, *gram)


def combine_kernel(plan, count, *refs):
    for out, pieces in zip(refs[count:], plan):
        row = 0
        for rows, terms in pieces:
            values = [refs[index][start : start + rows, :] for index, start in terms]
            while len(values) > 1:
                values = [sum(values[i + 1 : i + 2], values[i]) for i in range(0, len(values), 2)]
            out[row : row + rows, :] = values[0]
            row += rows


def combine(arrays, plan):
    shapes = [jax.ShapeDtypeStruct((sum(rows for rows, _ in pieces), TILE), jnp.float32) for pieces in plan]
    size = sum(shape.shape[0] for shape in shapes) * TILE
    return pl.pallas_call(
        functools.partial(combine_kernel, plan, len(arrays)),
        in_specs=[ON_CHIP] * len(arrays),
        out_specs=[ON_CHIP] * len(plan),
        out_shape=shapes,
        compiler_params=pltpu.CompilerParams(vmem_limit_bytes=SMALL),
        cost_estimate=pl.CostEstimate(flops=2 * size, bytes_accessed=12 * size, transcendentals=0),
        name="combine",
    )(*arrays)


def apply_inverse(parts, inverse, basis):
    high, low = split(inverse[...])
    start = 0
    for part in parts:
        size = part.shape[0]
        basis[start : start + size, :] = product(part[...], high, low).astype(jnp.bfloat16)
        start += size


def add_products(standard, basis, base, value):
    row = 0
    for first, count in base:
        size = count * TILE
        term = jnp.dot(
            standard[:, first * TILE : first * TILE + size],
            basis[row : row + size, :],
            preferred_element_type=jnp.float32,
        )
        value = term if value is None else value + term
        row += size
    return value


def begin_kernel(pieces, base, *refs):
    parts = refs[:pieces]
    inverse, standard, out, basis = refs[pieces:]
    apply_inverse(parts, inverse, basis)
    out[...] = add_products(standard, basis, base, None)


def begin_project(parts, base, inverse, standard):
    samples = standard.shape[0]
    rows = sum(part.shape[0] for part in parts)
    return pl.pallas_call(
        functools.partial(begin_kernel, len(parts), base),
        in_specs=[ON_CHIP] * (len(parts) + 2),
        out_specs=ON_CHIP,
        out_shape=jax.ShapeDtypeStruct((samples, TILE), jnp.float32),
        scratch_shapes=[pltpu.VMEM((rows, TILE), jnp.bfloat16)],
        compiler_params=pltpu.CompilerParams(vmem_limit_bytes=SMALL),
        cost_estimate=pl.CostEstimate(flops=2 * samples * rows * TILE, bytes_accessed=2 * samples * rows, transcendentals=0),
        name="begin_project",
    )(*parts, inverse, standard)


def project_kernel(pieces, base, *refs):
    parts = refs[:pieces]
    begun, inverse, standard, kept, projected, turned, gram, basis, whole = refs[pieces:]
    apply_inverse(parts, inverse, basis)
    value = add_products(standard, basis, base, begun[...])
    finish_rows(value, kept, projected, turned, whole)
    share_gram(whole, gram)


def project(parts, base, begun, inverse, standard, kept):
    samples = standard.shape[0]
    rows = sum(part.shape[0] for part in parts)
    return pl.pallas_call(
        functools.partial(project_kernel, len(parts), base),
        in_specs=[ON_CHIP] * (len(parts) + 4),
        out_specs=[ON_CHIP] * 3,
        out_shape=[
            jax.ShapeDtypeStruct((samples, TILE), jnp.bfloat16),
            jax.ShapeDtypeStruct((TILE, samples), jnp.bfloat16),
            jax.ShapeDtypeStruct((TILE, TILE), jnp.float32),
        ],
        scratch_shapes=[pltpu.VMEM((rows, TILE), jnp.bfloat16), pltpu.VMEM((TILE, TILE), jnp.float32)],
        compiler_params=pltpu.CompilerParams(vmem_limit_bytes=SMALL),
        cost_estimate=pl.CostEstimate(flops=2 * samples * rows * TILE, bytes_accessed=2 * samples * rows, transcendentals=0),
        name="project",
    )(*parts, begun, inverse, standard, kept)


PANEL = 16


def eliminate(first, last, left, right, out):
    panel_rows = lax.broadcasted_iota(jnp.int32, (PANEL, TILE), 0)
    for start in range(first, last, PANEL):
        stop = start + PANEL
        upper = left[start:stop, :]
        done = right[start:stop, :]
        columns = [
            jnp.broadcast_to(upper[:, start + j : start + j + 1], (PANEL, TILE)) for j in range(PANEL)
        ]
        for k in range(PANEL):
            pivot = columns[k][k : k + 1, :]
            root = lax.rsqrt(pivot)
            below = jnp.where(panel_rows > k, columns[k] * (root * root), 0.0)
            for j in range(k + 1, PANEL):
                columns[j] = columns[j] - below * columns[j][k : k + 1, :]
            factor = jnp.where(panel_rows == k, root, 1.0)
            upper = upper * factor - below * upper[k : k + 1, :]
            done = done * factor - below * done[k : k + 1, :]
        out[start:stop, :] = done
        if stop < TILE:
            left_parts = thirds(upper)
            right_parts = thirds(jnp.concatenate([upper, done], axis=1))
            pairs = ((0, 0), (0, 1), (1, 0), (0, 2), (1, 1), (2, 0))
            both = lax.dot_general(
                jnp.concatenate([left_parts[i] for i, _ in pairs], axis=0),
                jnp.concatenate([right_parts[j] for _, j in pairs], axis=0),
                (((0,), (0,)), ((), ())),
                preferred_element_type=jnp.float32,
            )
            left[stop:, :] -= both[stop:, :TILE]
            right[stop:, :] -= both[stop:, TILE:]


def begin_kernel_inverse(last, own, other, left, right):
    device = this_device()
    height = TILE // GROUPS
    for half, source in enumerate((own, other)):
        for row in range(GROUPS // 2):
            start = pl.multiple_of(group_at(device, half * (GROUPS // 2) + row) * height, height)
            left[pl.ds(start, height), :] = source[row * height : (row + 1) * height, :]
    lanes = lax.broadcasted_iota(jnp.int32, (TILE, TILE), 1)
    subs = lax.broadcasted_iota(jnp.int32, (TILE, TILE), 0)
    right[...] = jnp.where(lanes == subs, 1.0, 0.0)
    eliminate(0, last, left, right, right)


def end_kernel_inverse(first, left_in, right_in, out, left, right):
    left[first:, :] = left_in[first:, :]
    right[first:, :] = right_in[first:, :]
    out[:first, :] = right_in[:first, :]
    eliminate(first, TILE, left, right, out)


SQUARE = jax.ShapeDtypeStruct((TILE, TILE), jnp.float32)


def begin_inverse(last, own, other):
    return pl.pallas_call(
        functools.partial(begin_kernel_inverse, last),
        in_specs=[ON_CHIP, ON_CHIP],
        out_specs=[ON_CHIP, ON_CHIP],
        out_shape=[SQUARE, SQUARE],
        compiler_params=pltpu.CompilerParams(vmem_limit_bytes=SMALL),
        cost_estimate=pl.CostEstimate(flops=1_000_000_000, bytes_accessed=8_000_000, transcendentals=0),
        name="begin_inverse",
    )(own, other)


def end_inverse(first, left, right):
    return pl.pallas_call(
        functools.partial(end_kernel_inverse, first),
        in_specs=[ON_CHIP, ON_CHIP],
        out_specs=ON_CHIP,
        out_shape=SQUARE,
        scratch_shapes=[pltpu.VMEM((TILE, TILE), jnp.float32), pltpu.VMEM((TILE, TILE), jnp.float32)],
        compiler_params=pltpu.CompilerParams(vmem_limit_bytes=SMALL),
        cost_estimate=pl.CostEstimate(flops=1_000_000_000, bytes_accessed=8_000_000, transcendentals=0),
        name="end_inverse",
    )(left, right)


def invert_factor(own, other):
    return begin_inverse(TILE, own, other)[1]


def pick_kernel(keep, projected, chosen):
    samples = projected.shape[0]
    lanes = lax.broadcasted_iota(jnp.int32, (TILE, samples), 1).astype(jnp.float32)
    for j in range(keep.shape[0]):
        row = jnp.broadcast_to(keep[j : j + 1, :].astype(jnp.float32), (TILE, TILE)).T
        pick = jnp.where(lanes == jnp.tile(row, (1, samples // TILE)), 1.0, 0.0).astype(jnp.bfloat16)
        value = jnp.dot(pick, projected[...], preferred_element_type=jnp.float32)
        chosen[j * TILE : (j + 1) * TILE, :] = value.astype(jnp.bfloat16)


def pick_rows(keep, projected):
    return pl.pallas_call(
        pick_kernel,
        in_specs=[ON_CHIP, ON_CHIP],
        out_specs=ON_CHIP,
        out_shape=jax.ShapeDtypeStruct((keep.shape[0] * TILE, TILE), jnp.bfloat16),
        compiler_params=pltpu.CompilerParams(vmem_limit_bytes=SMALL),
        cost_estimate=pl.CostEstimate(flops=500_000_000, bytes_accessed=4_000_000, transcendentals=0),
        name="pick_rows",
    )(keep, projected)


def scores_kernel(scale, chosen, inverse, scores):
    high, low = split(inverse[...])
    dims = (((1,), (1,)), ((), ()))
    value = lax.dot_general(chosen[...], high, dims, preferred_element_type=jnp.float32)
    value = value + lax.dot_general(chosen[...], low, dims, preferred_element_type=jnp.float32)
    scores[...] = value * scale


def score(scale, chosen, inverse):
    return pl.pallas_call(
        functools.partial(scores_kernel, scale),
        out_shape=jax.ShapeDtypeStruct(chosen.shape, jnp.float32),
        compiler_params=pltpu.CompilerParams(vmem_limit_bytes=SMALL),
        cost_estimate=pl.CostEstimate(flops=500_000_000, bytes_accessed=4_000_000, transcendentals=0),
        name="score",
    )(chosen, inverse)


def loadings_kernel(pieces, positions, *refs):
    wide = lax.axis_index("wide") & 7
    parts = refs[:pieces]
    inverse, loadings = refs[pieces:]
    high, low = split(inverse[...])
    value = product(jnp.concatenate([part[...] for part in parts], axis=0), high, low)
    for i, position in enumerate(positions):
        place = wide ^ (((position & 3) << 1) | (position >> 2))
        start = pl.multiple_of(place * TILE, TILE)
        loadings[pl.ds(start, TILE), :] = value[i * TILE : (i + 1) * TILE, :]


def load(positions, parts, inverse):
    count = sum(part.shape[0] for part in parts)
    return pl.pallas_call(
        functools.partial(loadings_kernel, len(parts), positions),
        in_specs=[ON_CHIP] * (len(parts) + 1),
        out_shape=jax.ShapeDtypeStruct((count, TILE), jnp.float32),
        compiler_params=pltpu.CompilerParams(vmem_limit_bytes=VMEM),
        cost_estimate=pl.CostEstimate(flops=100_000_000, bytes_accessed=1_000_000, transcendentals=0),
        name="load",
    )(*parts, inverse)


def span(rows, *terms):
    return (rows, terms)


def scatter_sum(turned, standard, gram, far):
    four = 4 * TILE
    eight = 8 * TILE
    slot = TILE // GROUPS
    half = TILE // 2
    three = 3 * TILE
    far = exchange(far, core_mask)
    upper = totals(turned, standard, 8, 16)
    send, send_rest = combine(
        [upper, far, gram],
        [
            [span(three, (0, four + TILE), (1, four + TILE)), span(half, (2, 0), (1, eight))],
            [span(four + TILE, (0, 0), (1, 0))],
        ],
    )
    first = exchange(send, first_mask)
    rest = exchange(send_rest, first_mask)
    close = exchange(totals(turned, standard, 16, 24), core_mask)
    own = totals(turned, standard, 0, 8)
    (send_next,) = combine(
        [own, close, first, send],
        [[span(three, (0, four + TILE), (1, four + TILE), (2, 0)), span(half, (3, three), (2, three))]],
    )
    second = exchange(send_next, second_mask)
    (send_last,) = combine([own, close, rest], [[span(TILE, (0, four), (1, four), (2, four))]])
    last = exchange(send_last, second_mask)

    def share(q):
        return span(slot, (4, three + q * slot), (3, three + q * slot))

    def packet(q):
        start = q * TILE
        return [span(TILE, (0, start), (1, start), (2, start), (3, start - TILE)), share(q)]

    *packets, own_share = combine(
        [own, close, rest, second, send_next], [packet(q) for q in (3, 2, 1)] + [[share(0)]]
    )
    arrived = [exchange(packet, lambda d, q=q: (3 - q) << 3) for q, packet in enumerate(packets)]
    block = span(TILE, *((i, 0) for i in (0, 1, 2, 3, 5, 6, 7)))
    part = span(slot, (4, 0), (7, TILE), (6, TILE), (5, TILE))
    packet, total = combine([own, close, rest, last, own_share] + arrived, [[block, part], [block]])
    if lax.axis_size(AXES) == BLOCKS:
        return packet, total
    packet = across_rest(packet)
    return packet, packet[:TILE]


def across_rest(value):
    bit = BLOCKS
    while bit < lax.axis_size(AXES):
        value = value + exchange(value, lambda d, bit=bit: bit)
        bit *= 2
    return value


def along_z(value):
    return [exchange(value, lambda d, q=q: q << 3) for q in range(1, 4)]


def gather_near(packet):
    slot = TILE // GROUPS
    return combine(
        [packet] + along_z(packet),
        [[span(TILE, (q, 0)) for q in range(4)], [span(slot, (q, TILE)) for q in range(4)]],
    )


def gather_last(packet):
    slot = TILE // GROUPS
    return combine(
        [packet] + along_z(packet),
        [[span(TILE, (q, 0)) for q in (1, 2, 3)], [span(slot, (q, TILE)) for q in range(4)]],
    )


def on_device(dosage, keep_rows, allele_counts, projection):
    groups = lax.axis_size(AXES)
    samples_total = dosage.shape[0] * groups
    kept_total = keep_rows.shape[0] * groups
    keep = keep_rows.reshape(-1, TILE)
    counts = allele_counts.reshape(-1, TILE)
    standard, _, turned, gram, kept, far = standardize(samples_total, dosage, keep, counts, projection)
    packet, _ = scatter_sum(turned, standard, gram, far)
    near, share = gather_near(packet)
    across = exchange(near, second_mask)
    other = exchange(share, core_mask)
    later, other = lax.optimization_barrier((near, other))
    along = exchange(later, first_mask)
    middle = begin_inverse(SPLIT, share, other)
    across, middle = lax.optimization_barrier((across, middle))
    corner = exchange(across, first_mask)
    inverse = end_inverse(SPLIT, *middle)
    early = [near, across, along] + [exchange(part, core_mask) for part in (near, across)]
    begun = begin_project(early, [(0, 4), (4, 4), (8, 4), (16, 4), (20, 4)], inverse, standard)
    corner, begun = lax.optimization_barrier((corner, begun))
    late = [exchange(along, core_mask), corner, exchange(corner, core_mask)]
    ranges = [(24, 4), (12, 4), (28, 4)]
    projected, turned, gram = project(late, ranges, begun, inverse, standard, kept)
    packet, total = scatter_sum(turned, standard, gram, totals(turned, standard, 24, 32, gram))
    chosen = pick_rows(keep, projected)
    packet, total, chosen = lax.optimization_barrier((packet, total, chosen))
    first_beside = exchange(total, lambda d: 4)
    near, share = gather_last(packet)
    beside = exchange(near, lambda d: 4)
    other, first_beside = lax.optimization_barrier((exchange(share, core_mask), first_beside))
    inverse = invert_factor(share, other)
    scores = score(math.sqrt(kept_total), chosen, inverse)
    loadings = load((0, 4, 1, 2, 3, 5, 6, 7), [total, first_beside, near, beside], inverse)
    return (scores, loadings)


def solution(mesh):
    in_specs = (P(AXES, None), P(AXES), P(), P())
    out_specs = (P(AXES, None), P("narrow", None))
    return jax.shard_map(
        on_device, mesh=mesh, in_specs=in_specs, out_specs=out_specs, check_vma=False
    )
```
